256 devices in a mesh: ctx: 32 (over z_hi, y, core), head: 8 (over x, z_lo).
Axes of the slice: x: 4, y: 4, z: 8 (z_hi: 4, z_lo: 2; z = z_hi * 2 + z_lo), core: 2. Of those that a mesh axis runs over, the one named last changes fastest.
Arguments:
- query_set: bfloat16 [3, 8192, 2048], P(None, ('ctx', 'head')), may hold values from -80 to 80
- key_set: bfloat16 [3, 8192, 2048], P(None, ('ctx', 'head')), may hold values from -80 to 80
- value_set: bfloat16 [3, 8192, 2048], P(None, ('ctx', 'head')), may hold values from -6 to 6
- block_order: int32 [64], replicated, may hold values from 0 to 63, each once
- documents: int32 [8192], replicated, may hold values from 0 to 3, as said below
Outputs:
- attended: bfloat16 [3, 8192, 2048], P(None, ('ctx', 'head'))
The draws below stay inside these ranges and needn't reach their ends.
Inputs may be any that keep to these rules, and one draw needn't show every extreme that they name: `block_order`: a permutation. Never falling along the sequence; four documents, each non-empty.
All inputs are finite; a program needn't handle non-finite values.
Results may differ from the reference program's by a relative error of at most 0.013.
Values may be sent and summed in bfloat16 or wider, within the bound.
No kernel may reach another device: no remote copies, remote signals or barrier semaphores. Data moves between devices by JAX's collectives and lax.ppermute only.
A program may use at most 192 MiB of HBM per device.

```python
import jax
import jax.numpy as jnp
from jax import lax

HD = 128
HQ = 16
TOK_DEV = 256
GROUP = 128
SEQ = 8192
WIDTH = 2048
N_CTX = 32


def drawn_draw(key):
    noise_key = jax.random.fold_in(key, 0)
    fresh = jnp.clip(jax.random.normal(noise_key, (3, SEQ, HQ * HD), jnp.float32), -6.0, 6.0)
    return jnp.clip(fresh, -80.0, 80.0).astype(jnp.bfloat16)


def draw_query_set(key, part):
    key = jax.random.fold_in(key, 1)
    return drawn_draw(key)


def draw_key_set(key, part):
    key = jax.random.fold_in(key, 2)
    return drawn_draw(key)


def draw_documents(key, part):
    key = jax.random.fold_in(key, 3)
    eighth = SEQ // 8
    lows = jnp.array([1, 3, 5], jnp.int32) * eighth
    offsets = jax.random.randint(key, (3,), 0, 2 * eighth, jnp.int32)
    cuts = lows + offsets
    positions = jnp.arange(SEQ, dtype=jnp.int32)
    return jnp.sum((positions[:, None] >= cuts[None, :]).astype(jnp.int32), axis=1).astype(jnp.int32)


def block_scale(stream_key, dims, pieces, smallest, largest):
    gain = 1.0
    for position, blocks in pieces:
        steps = jax.random.uniform(jax.random.fold_in(jax.random.fold_in(stream_key, 6), position), (blocks,), jnp.float32, smallest / len(pieces), largest / len(pieces))
        gain = gain * jnp.repeat(jnp.exp(steps), dims[position] // blocks).reshape((-1,) + (1,) * (len(dims) - 1 - position))
    return gain


def noise(stream_key, dims, deviation, limit, shards=(), kind=jnp.bfloat16):
    values = deviation * jax.random.normal(stream_key, dims, jnp.float32)
    if shards:
        values = values * block_scale(stream_key, dims, shards, -0.22, 0.18)
    return jnp.clip(values, -limit, limit).astype(kind)


def setup_inputs(seed: int = 0) -> dict:
    key_list = jax.random.split(jax.random.key(seed), 6)
    query_set = draw_query_set(jax.random.fold_in(key_list[5], 71), 0)
    key_set = draw_key_set(jax.random.fold_in(key_list[5], 71), 0)
    value_set = noise(key_list[2], (3, SEQ, WIDTH), 1.0, 6.0, ((1, 256),))
    block_order = jax.random.permutation(key_list[3], 2 * N_CTX).astype(jnp.int32)
    documents = draw_documents(jax.random.fold_in(key_list[5], 71), 0)
    return {"query_set": query_set, "key_set": key_set, "value_set": value_set, "block_order": block_order, "documents": documents}


def reference(query_set, key_set, value_set, block_order, documents):
    pos = (block_order[:, None] * GROUP + jnp.arange(GROUP, dtype=jnp.int32)[None, :]).reshape(-1).astype(jnp.int32)
    doc = documents[pos]
    scale = 1.0 / (HD ** 0.5)
    qall = query_set.astype(jnp.float32).reshape(3, SEQ, HQ, HD)
    kall = key_set.astype(jnp.float32).reshape(3, SEQ, HQ, HD)
    vall = value_set.astype(jnp.float32).reshape(3, SEQ, HQ, HD)
    blocks = SEQ // TOK_DEV

    def one_head(head):
        qh = qall[:, :, head, :]
        kh = kall[:, :, head, :]
        vh = vall[:, :, head, :]

        def one_block(block):
            first = (block * TOK_DEV).astype(jnp.int32)
            qb = lax.dynamic_slice_in_dim(qh, first, TOK_DEV, 1)
            qpos = lax.dynamic_slice_in_dim(pos, first, TOK_DEV, 0)
            qdoc = lax.dynamic_slice_in_dim(doc, first, TOK_DEV, 0)
            hi = lax.Precision.HIGHEST
            scores = jnp.dot(qb[0], kh[0].T, precision=hi) * scale
            visible = (pos[None, :] <= qpos[:, None]) & (doc[None, :] == qdoc[:, None])
            masked = jnp.where(visible, scores, -1e30)
            top = jnp.max(masked, axis=1, keepdims=True)
            expo = jnp.where(visible, jnp.exp(masked - top), 0.0)
            total = jnp.sum(expo, axis=1, keepdims=True)
            rounded = lax.optimization_barrier(expo.astype(jnp.bfloat16)).astype(jnp.float32)
            numer = jnp.dot(rounded, vh[0], precision=hi)
            primal = numer / total
            result = [primal]
            for idx in (1, 2):
                dscore = (jnp.dot(qb[idx], kh[0].T, precision=hi) + jnp.dot(qb[0], kh[idx].T, precision=hi)) * scale
                weighted = expo * dscore
                cterm = jnp.sum(weighted, axis=1, keepdims=True)
                wround = lax.optimization_barrier(weighted.astype(jnp.bfloat16)).astype(jnp.float32)
                grad = jnp.dot(wround, vh[0], precision=hi) + jnp.dot(rounded, vh[idx], precision=hi)
                result.append(grad / total - (cterm / total) * primal)
            return jnp.stack(result, 0).astype(jnp.bfloat16)

        return lax.map(one_block, jnp.arange(blocks, dtype=jnp.int32))

    outs = lax.map(one_head, jnp.arange(HQ, dtype=jnp.int32))
    outs = jnp.transpose(outs, (2, 1, 3, 0, 4)).reshape(3, SEQ, HQ * HD)
    return outs
```

```python
import jax
import jax.numpy as jnp
from jax import lax
from jax.experimental import pallas as pl
from jax.experimental.pallas import tpu as pltpu
from jax.sharding import Mesh
from jax.sharding import PartitionSpec as P

HD = 128
HEADS = 16
BLOCK = 128
SLICE = 32
Z = ("zh", "zl")
XY = ("y", "xh", "xl")
NAMES = ("zh", "y", "c", "xh", "xl", "zl")
SIZES = (4, 4, 2, 2, 2, 2)
NZ = 8
SCALE = 1.0 / HD**0.5
LOG2E = 1.4426950408889634
HIDDEN = -1e30
VMEM = pl.BlockSpec(memory_space=pltpu.VMEM)
SMEM = pl.BlockSpec(memory_space=pltpu.SMEM)
ANY = pl.BlockSpec(memory_space=pl.ANY)

KRANK = 0
KPOS = 32
QRANK = 64
QPOS = 80
QINDEX = 96
KLO = 112
KHI = 120
STARTS = 128
ZPOS = 131
ZLOW = 132
N_SCALARS = 133

QT = 128
KT = 256


def split_heads(*arrays):
    def kernel(*refs):
        out = refs[-1]
        for h in range(HEADS):
            for a, ref in enumerate(refs[:-1]):
                out[h, 3 * a : 3 * a + 3] = ref[:, :, h * HD : (h + 1) * HD]

    return pl.pallas_call(
        kernel,
        out_shape=jax.ShapeDtypeStruct((HEADS, 3 * len(arrays), SLICE, HD), jnp.bfloat16),
        in_specs=[VMEM] * len(arrays),
        out_specs=VMEM,
    )(*arrays)


def join_heads(parts):
    def kernel(ref, out):
        for h in range(HEADS):
            out[:, :, h * HD : (h + 1) * HD] = ref[h]

    return pl.pallas_call(
        kernel,
        out_shape=jax.ShapeDtypeStruct((3, SLICE, HEADS * HD), jnp.bfloat16),
        in_specs=[VMEM],
        out_specs=VMEM,
    )(parts)


def ranks(values):
    n = values.shape[0]
    order = jnp.sum((values[None, :] < values[:, None]).astype(jnp.int32), axis=1)
    hits = order[None, :] == jnp.arange(n, dtype=jnp.int32)[:, None]
    index = jnp.sum(jnp.where(hits, jnp.arange(n, dtype=jnp.int32)[None, :], 0), axis=1)
    ordered = jnp.sum(jnp.where(hits, values[None, :], 0), axis=1)
    return order, index, ordered


def scalars(order, documents):
    zh, zl, c = lax.axis_index("zh"), lax.axis_index("zl"), lax.axis_index("c")
    blocks = order.reshape(4, 4, 2, 2)
    mine = lax.dynamic_index_in_dim(blocks, c, 2, keepdims=False)
    here = lax.dynamic_index_in_dim(blocks, zh, 0, keepdims=False)
    own = lax.dynamic_index_in_dim(here, c, 1, keepdims=False).reshape(-1)
    other = lax.dynamic_index_in_dim(here, 1 - c, 1, keepdims=False).reshape(-1)
    krank, _, kpos = ranks(mine.reshape(-1))
    qrank, qindex, qpos = ranks(jnp.concatenate([own, other]))
    starts = jnp.sum(
        (documents[None, :] < jnp.arange(1, 4, dtype=jnp.int32)[:, None]).astype(jnp.int32), axis=1
    )
    first = qpos[0::2] * BLOCK
    last = qpos[1::2] * BLOCK + BLOCK - 1
    begin = jnp.max(jnp.where(starts[None, :] <= first[:, None], starts[None, :], 0), axis=1)
    below = jnp.sum((kpos[None, :] * BLOCK + BLOCK - 1 < begin[:, None]).astype(jnp.int32), axis=1)
    upto = jnp.sum((kpos[None, :] * BLOCK <= last[:, None]).astype(jnp.int32), axis=1)
    return jnp.concatenate(
        [krank, kpos, qrank, qpos, qindex, below // 2, (upto + 1) // 2, starts,
         jnp.stack([zh * 2 + zl, zl]).astype(jnp.int32)]
    )


def attention(sc, queries, pieces):
    keys = sorted(pieces)

    def kernel(sc, q_own, q_other, *refs):
        n = len(keys)
        kv_refs, (out_own, out_other), (kv, q, s_all, sem) = refs[:n], refs[n : n + 2], refs[n + 2 :]
        copies = []
        for i, q_ref in enumerate((q_own, q_other)):
            for b in range(8):
                copies.append((q_ref.at[b], q.at[sc[QRANK + i * 8 + b]]))
        for (half, offset), ref in zip(keys, kv_refs, strict=True):
            z = lax.rem(sc[ZPOS] + offset + NZ, NZ)
            zh, zl = z // 2, lax.rem(z, 2)
            for b in range(4):
                copies.append((ref.at[b], kv.at[sc[KRANK + zh * 8 + half * 4 + b], zl]))
        started = [pltpu.make_async_copy(src, dst, sem) for src, dst in copies]
        for copy in started:
            copy.start()
        for copy in started:
            copy.wait()

        row = lax.broadcasted_iota(jnp.int32, (QT, 1), 0)
        in_row = lax.rem(row, 64)
        row_offset = (in_row // SLICE * 2 + sc[ZLOW]) * SLICE + lax.rem(row, SLICE)
        col = lax.broadcasted_iota(jnp.int32, (1, KT), 1)
        in_col = lax.rem(col, BLOCK)
        col_offset = (lax.rem(in_col, 64) // SLICE * 2 + in_col // 64) * SLICE + lax.rem(col, SLICE)
        lane = lax.broadcasted_iota(jnp.int32, (64, HD), 1)
        nt = (((1,), (1,)), ((), ()))

        def key_tile(kt, t):
            return kv[pl.ds(2 * kt, 2), :, :, t].reshape(KT, HD)

        def tile(qt, _):
            q0, q1, q2 = (q[pl.ds(2 * qt, 2), :, t].reshape(QT, HD) for t in range(3))
            q10 = jnp.concatenate([q1, q0], 1)
            q20 = jnp.concatenate([q2, q0], 1)
            qpos = jnp.where(row < 64, sc[QPOS + 2 * qt], sc[QPOS + 2 * qt + 1]) * BLOCK + row_offset
            qstart = jnp.zeros_like(qpos)
            for d in range(3):
                qstart = jnp.where(qpos >= sc[STARTS + d], sc[STARTS + d], qstart)
            lo, hi = sc[KLO + qt], sc[KHI + qt]

            def scores(kt, top):
                kpos = jnp.where(col < BLOCK, sc[KPOS + 2 * kt], sc[KPOS + 2 * kt + 1]) * BLOCK + col_offset
                s = lax.dot_general(q0, key_tile(kt, 0), nt, preferred_element_type=jnp.float32)
                s = jnp.where((kpos <= qpos) & (kpos >= qstart), s, HIDDEN)
                s_all[kt] = s
                return jnp.maximum(top, jnp.maximum(s[:, :HD], s[:, HD:]))

            top = lax.fori_loop(lo, hi, scores, jnp.full((QT, HD), HIDDEN, jnp.float32))
            top = jnp.max(top, axis=1, keepdims=True)
            shift = jnp.where(top < 0.5 * HIDDEN, 0.0, top)

            def weigh(kt, state):
                total, c1, c2, acc, acc_w = state
                e = jnp.exp2((s_all[kt] - shift) * (SCALE * LOG2E))
                es = e * SCALE
                k0, k1, k2 = (key_tile(kt, t) for t in range(3))
                d1 = lax.dot_general(q10, jnp.concatenate([k0, k1], 1), nt, preferred_element_type=jnp.float32)
                d2 = lax.dot_general(q20, jnp.concatenate([k0, k2], 1), nt, preferred_element_type=jnp.float32)
                w1, w2 = es * d1, es * d2
                v = jnp.concatenate([key_tile(kt, t) for t in (3, 4, 5)], 1)
                acc = acc + jnp.dot(e.astype(jnp.bfloat16), v, preferred_element_type=jnp.float32)
                w = jnp.concatenate([w1.astype(jnp.bfloat16), w2.astype(jnp.bfloat16)], 0)
                acc_w = acc_w + jnp.dot(w, v[:, :HD], preferred_element_type=jnp.float32)
                return (
                    total + (e[:, :HD] + e[:, HD:]),
                    c1 + (w1[:, :HD] + w1[:, HD:]),
                    c2 + (w2[:, :HD] + w2[:, HD:]),
                    acc,
                    acc_w,
                )

            zero = jnp.zeros((QT, HD), jnp.float32)
            total, c1, c2, acc, acc_w = lax.fori_loop(
                lo, hi, weigh,
                (zero, zero, zero, jnp.zeros((QT, 3 * HD), jnp.float32), jnp.zeros((2 * QT, HD), jnp.float32)),
            )
            total, c1, c2 = (jnp.sum(v, axis=1, keepdims=True) for v in (total, c1, c2))
            results = (acc[:, :HD], acc[:, HD : 2 * HD] + acc_w[:QT], acc[:, 2 * HD :] + acc_w[QT:])

            for half in range(2):
                rows = slice(64 * half, 64 * half + 64)
                stats = jnp.where(
                    lane == 0, top[rows],
                    jnp.where(lane == 1, total[rows], jnp.where(lane == 2, c1[rows], c2[rows])),
                )
                block = [r.reshape(2, SLICE, HD) for r in (*(r[rows] for r in results), stats)]
                index = sc[QINDEX + 2 * qt + half]

                @pl.when(index < 8)
                def _(block=block, index=index):
                    for t in range(4):
                        out_own[index, :, t] = block[t]

                @pl.when(index >= 8)
                def _(block=block, index=index):
                    for t in range(4):
                        out_other[index - 8, :, t] = block[t]

            return 0

        lax.fori_loop(0, 8, tile, 0)

    part = jax.ShapeDtypeStruct((8, 2, 4, SLICE, HD), jnp.float32)
    return pl.pallas_call(
        kernel,
        out_shape=(part, part),
        in_specs=[SMEM] + [ANY] * (2 + len(keys)),
        out_specs=(VMEM, VMEM),
        scratch_shapes=[
            pltpu.VMEM((32, 2, 2, 6, SLICE, HD), jnp.bfloat16),
            pltpu.VMEM((16, 2, 3, SLICE, HD), jnp.bfloat16),
            pltpu.VMEM((16, QT, KT), jnp.float32),
            pltpu.SemaphoreType.DMA,
        ],
        compiler_params=pltpu.CompilerParams(vmem_limit_bytes=32 * 2**20),
    )(sc, *queries, *(pieces[k] for k in keys))


def merge(mine, theirs):
    def kernel(a, b, out):
        for blk in range(8):
            for xl in range(2):
                sa, sb = a[blk, xl, 3], b[blk, xl, 3]
                ta, tb = sa[:, 0:1], sb[:, 0:1]
                top = jnp.maximum(ta, tb)
                fa = jnp.exp2((ta - top) * (SCALE * LOG2E))
                fb = jnp.exp2((tb - top) * (SCALE * LOG2E))
                total, c1, c2 = (sa[:, i : i + 1] * fa + sb[:, i : i + 1] * fb for i in (1, 2, 3))
                inv = 1.0 / total
                fa, fb = fa * inv, fb * inv
                primal = a[blk, xl, 0] * fa + b[blk, xl, 0] * fb
                out[blk * 2 + xl, 0] = primal.astype(jnp.bfloat16)
                for i, c in ((1, c1), (2, c2)):
                    grad = a[blk, xl, i] * fa + b[blk, xl, i] * fb
                    out[blk * 2 + xl, i] = (grad - (c * inv) * primal).astype(jnp.bfloat16)

    return pl.pallas_call(
        kernel,
        out_shape=jax.ShapeDtypeStruct((16, 3, SLICE, HD), jnp.bfloat16),
        in_specs=[VMEM, VMEM],
        out_specs=VMEM,
    )(mine, theirs)


def hop(block, direction):
    return lax.ppermute(block, Z, [(i, (i + direction) % NZ) for i in range(NZ)])


def swap_cores(block):
    return lax.ppermute(block, "c", [(0, 1), (1, 0)])


def shards(query_set, key_set, value_set, block_order, documents):
    kv = lax.all_to_all(split_heads(key_set, value_set), XY, 0, 0)
    kv = kv.reshape(8, 2, 6, SLICE, HD)
    q = lax.all_to_all(split_heads(query_set), XY, 0, 0).reshape(8, 2, 3, SLICE, HD)
    pieces = {(half, 0): kv[4 * half : 4 * half + 4] for half in range(2)}
    ups = [pieces[0, 0], pieces[1, 0]]
    downs = [pieces[0, 0], pieces[1, 0]]
    for step in range(1, 5):
        for half in range(2):
            if step < 4 or half == 0:
                ups[half] = pieces[half, -step] = hop(ups[half], 1)
            if step < 4 or half == 1:
                downs[half] = pieces[half, step] = hop(downs[half], -1)
    sc = scalars(block_order, documents)
    own, other = attention(sc, (q, swap_cores(q)), pieces)
    done = merge(own, swap_cores(other))
    return join_heads(lax.all_to_all(done, XY, 0, 0))


def solution(mesh):
    fine = Mesh(mesh.devices.reshape(SIZES), NAMES)
    rows = P(None, NAMES, None)
    return jax.shard_map(
        shards,
        mesh=fine,
        in_specs=(rows, rows, rows, P(), P()),
        out_specs=rows,
        check_vma=False,
    )
```

```python
import jax
import jax.numpy as jnp
from jax import lax
from jax.experimental import pallas as pl
from jax.experimental.pallas import tpu as pltpu
from jax.sharding import Mesh
from jax.sharding import PartitionSpec as P

HD = 128
HEADS = 16
BLOCK = 128
SLICE = 32
HALF = 2 * SLICE
Z = ("zh", "zl")
XY = ("y", "xh", "xl")
NAMES = ("zh", "y", "c", "xh", "xl", "zl")
SIZES = (4, 4, 2, 2, 2, 2)
NZ = 8
SCALE = 1.0 / HD**0.5
EXPONENT = SCALE * 1.4426950408889634
HIDDEN = -1e30
VMEM = pl.BlockSpec(memory_space=pltpu.VMEM)
SMEM = pl.BlockSpec(memory_space=pltpu.SMEM)
ANY = pl.BlockSpec(memory_space=pl.ANY)
NT = (((1,), (1,)), ((), ()))

NEAR = (-2, -1, 0, 1, 2)
NEXT = (-3, 3)
FIRST = (0, 40, 56, 72, 88, 96)
N_SLOTS = 96
QB, KB = 4, 8
QT, KT = QB * HALF, KB * HALF
INDEX, BASE, LOW, HIGH, STARTS = 0, 96, 192, 210, 228


def split_heads(*arrays):
    def kernel(*refs):
        out = refs[-1]
        for h in range(HEADS):
            for a, ref in enumerate(refs[:-1]):
                out[h, 3 * a : 3 * a + 3] = ref[:, :, h * HD : (h + 1) * HD]

    return pl.pallas_call(
        kernel,
        out_shape=jax.ShapeDtypeStruct((HEADS, 3 * len(arrays), SLICE, HD), jnp.bfloat16),
        in_specs=[VMEM] * len(arrays),
        out_specs=VMEM,
    )(*arrays)


def join_heads(parts):
    def kernel(ref, out):
        for h in range(HEADS):
            out[:, :, h * HD : (h + 1) * HD] = ref[h]

    return pl.pallas_call(
        kernel,
        out_shape=jax.ShapeDtypeStruct((3, SLICE, HEADS * HD), jnp.bfloat16),
        in_specs=[VMEM],
        out_specs=VMEM,
    )(parts)


def scalars(order, documents, zh, zl, c):
    i32 = jnp.int32
    z = zh * 2 + zl
    offsets = jnp.array((*NEAR, *NEXT, 4, 4, 0, 0, 0), i32)
    cores = jnp.array((0, 0, 0, 0, 0, 0, 0, 0, 1, 0, 1, 0), i32)
    sets = jnp.array((0, 0, 0, 0, 0, 1, 1, 2, 2, 3, 3, 4), i32)
    begins = jnp.array((0, 0, 0, 0, 0, 5, 5, 7, 7, 9, 9, 11), i32)
    planes = lax.rem(z + offsets + NZ, NZ)
    table = order.reshape(4, 4, 2, 2).transpose(0, 2, 1, 3).reshape(8, 8)
    line = planes // 2 * 2 + lax.rem(cores + c, 2)
    hit = line[:, None] == jnp.arange(8, dtype=i32)[None, :]
    pos = jnp.sum(jnp.where(hit[:, :, None], table[None], 0), axis=1)
    code = (sets[:, None] * 4096 + pos * 2 + lax.rem(planes, 2)[:, None]).reshape(-1)
    payload = ((jnp.arange(12, dtype=i32) - begins)[:, None] * 8 + jnp.arange(8, dtype=i32)[None, :]).reshape(-1)
    rank = jnp.sum((code[None, :] < code[:, None]).astype(i32), axis=1)
    slot = jnp.arange(N_SLOTS, dtype=i32)
    hits = rank[None, :] == slot[:, None]
    index = jnp.sum(jnp.where(hits, payload[None, :], 0), axis=1)
    low_bits = code % 4096
    base_of = low_bits // 2 * BLOCK + low_bits % 2 * SLICE
    base = jnp.sum(jnp.where(hits, base_of[None, :], 0), axis=1)
    starts = jnp.sum((documents[None, :] < jnp.arange(1, 4, dtype=i32)[:, None]).astype(i32), axis=1)
    first = base[FIRST[3] :: QB]
    last = base[FIRST[3] + QB - 1 :: QB] + BLOCK - SLICE
    begin = jnp.max(jnp.where(starts[None, :] <= first[:, None], starts[None, :], 0), axis=1)
    set_of = code // 4096
    member = set_of[None, None, :] == jnp.arange(3, dtype=i32)[:, None, None]
    before = base_of[None, None, :] + BLOCK - SLICE <= begin[None, :, None]
    upto = base_of[None, None, :] < last[None, :, None]
    low = jnp.sum((member & before).astype(i32), axis=2) // KB
    high = (jnp.sum((member & upto).astype(i32), axis=2) + KB - 1) // KB
    return jnp.concatenate([index, base, low.reshape(-1), high.reshape(-1), starts])


def lookup(sc, at, count, position, size):
    out = sc[at]
    for i in range(1, count):
        out = jnp.where(position >= i * size, sc[at + i], out)
    return out


def within(position):
    return lax.rem(position, HALF) // SLICE * HALF + lax.rem(position, SLICE)


def gathered(sc, ref, at, count, t):
    return jnp.concatenate([ref[sc[at + i], :, t].reshape(HALF, HD) for i in range(count)], 0)


def query_tile(sc, q, first, tile):
    at = first + tile * QB
    q0, q1, q2 = (gathered(sc, q, INDEX + at, QB, t) for t in range(3))
    row = lax.broadcasted_iota(jnp.int32, (QT, 1), 0)
    qpos = lookup(sc, BASE + at, QB, row, HALF) + within(row)
    start = jnp.zeros_like(qpos)
    for d in range(3):
        start = jnp.where(qpos >= sc[STARTS + d], sc[STARTS + d], start)
    return q0, jnp.concatenate([q1, q0], 1), jnp.concatenate([q2, q0], 1), qpos, start


def see(sc, kv, first, queries, state, low, high):
    q0, q10, q20, qpos, start = queries
    col = lax.broadcasted_iota(jnp.int32, (1, KT), 1)
    ones = jnp.ones((KT, HD), jnp.bfloat16)

    def step(kt, state):
        top, acc, acc_w = state
        at = first + kt * KB
        k0, k1, k2, v0, v1, v2 = (gathered(sc, kv, INDEX + at, KB, t) for t in range(6))
        kpos = lookup(sc, BASE + at, KB, col, HALF) + within(col)
        s = lax.dot_general(q0, k0, NT, preferred_element_type=jnp.float32)
        d1 = lax.dot_general(q10, jnp.concatenate([k0, k1], 1), NT, preferred_element_type=jnp.float32)
        d2 = lax.dot_general(q20, jnp.concatenate([k0, k2], 1), NT, preferred_element_type=jnp.float32)
        s = jnp.where((kpos <= qpos) & (kpos >= start), s, HIDDEN)
        peak = jnp.maximum(jnp.maximum(s[:, :HD], s[:, HD : 2 * HD]), jnp.maximum(s[:, 2 * HD : 3 * HD], s[:, 3 * HD :]))
        new = jnp.maximum(top, jnp.max(peak, axis=1, keepdims=True))
        shrink = jnp.exp2((top - new) * EXPONENT)
        shift = jnp.where(new < 0.5 * HIDDEN, 0.0, new)[:, :1]
        e = jnp.exp2((s - shift) * EXPONENT)
        w = jnp.concatenate([(e * d1).astype(jnp.bfloat16), (e * d2).astype(jnp.bfloat16)], 0)
        shrink4 = jnp.concatenate([shrink] * 4, 1)
        shrink2 = shrink4[:, : 2 * HD]
        acc = acc * shrink4 + jnp.dot(
            e.astype(jnp.bfloat16), jnp.concatenate([v0, v1, v2, ones], 1), preferred_element_type=jnp.float32
        )
        acc_w = acc_w * jnp.concatenate([shrink2, shrink2], 0) + jnp.dot(
            w, jnp.concatenate([v0, ones], 1), preferred_element_type=jnp.float32
        )
        return new, acc, acc_w

    return lax.fori_loop(low, high, step, state)


def fresh():
    return (
        jnp.full((QT, HD), HIDDEN, jnp.float32),
        jnp.zeros((QT, 4 * HD), jnp.float32),
        jnp.zeros((2 * QT, 2 * HD), jnp.float32),
    )


def pack_state(state):
    top, acc, acc_w = state
    total, c1, c2 = acc[:, 3 * HD :], acc_w[:QT, HD:] * SCALE, acc_w[QT:, HD:] * SCALE
    lane = lax.broadcasted_iota(jnp.int32, (QT, HD), 1)
    stats = jnp.where(lane == 0, top, jnp.where(lane == 1, total, jnp.where(lane == 2, c1, c2)))
    return (
        acc[:, :HD],
        acc[:, HD : 2 * HD] + acc_w[:QT, :HD] * SCALE,
        acc[:, 2 * HD : 3 * HD] + acc_w[QT:, :HD] * SCALE,
        stats,
    )


def unpack_state(parts):
    a, g1, g2, stats = parts
    top, total, c1, c2 = (jnp.broadcast_to(stats[:, i : i + 1], (QT, HD)) for i in range(4))
    zero = jnp.zeros((QT, HD), jnp.float32)
    acc = jnp.concatenate([a, g1, g2, total], 1)
    c = jnp.concatenate([c1, c2], 0) * (1.0 / SCALE)
    return top, acc, jnp.concatenate([jnp.concatenate([zero, zero], 0), c], 1)


def join_states(one, two):
    top = jnp.maximum(one[0], two[0])
    f, g = (jnp.exp2((t - top) * EXPONENT) for t in (one[0], two[0]))
    f4, g4 = (jnp.concatenate([v] * 4, 1) for v in (f, g))
    f2, g2 = (jnp.concatenate([v[:, : 2 * HD]] * 2, 0) for v in (f4, g4))
    return top, one[1] * f4 + two[1] * g4, one[2] * f2 + two[2] * g2


def gather_state(sc, ref, at):
    return unpack_state([gathered(sc, ref, at, QB, t) for t in range(4)])


def copy_in(pairs, sem):
    copies = [pltpu.make_async_copy(src, dst, sem) for src, dst in pairs]
    for copy in copies:
        copy.start()
    for copy in copies:
        copy.wait()


def attend(sc, queries, pieces, key_set, held=None):
    n = len(pieces)
    planes = n // 2

    def kernel(sc, q_own, q_other, *refs):
        kv_refs, refs = refs[:n], refs[n:]
        if held is not None:
            held_refs, refs = refs[:2], refs[2:]
        out_refs, (kv, q, st, sem) = refs[:2], refs[2:]
        pairs = [(q_own, q.at[0:8]), (q_other, q.at[8:16])]
        for i, ref in enumerate(kv_refs):
            pairs.append((ref, kv.at[i * 4 : i * 4 + 4]))
        if held is not None:
            pairs += [(ref, st.at[8 * i : 8 * i + 8]) for i, ref in enumerate(held_refs)]
        copy_in(pairs, sem)

        def tile(qt, _):
            info = query_tile(sc, q, FIRST[3], qt)
            low, high = sc[LOW + key_set * 6 + qt], sc[HIGH + key_set * 6 + qt]
            at = INDEX + FIRST[3] + qt * QB

            def work():
                before = fresh() if held is None else gather_state(sc, st, at)
                parts = pack_state(see(sc, kv, FIRST[key_set], info, before, low, high))
                for i in range(QB):
                    for t in range(4):
                        st[sc[at + i], :, t] = parts[t][i * HALF : i * HALF + HALF].reshape(2, SLICE, HD)

            if held is None:
                work()
            else:
                pl.when(high > low)(work)
            return 0

        lax.fori_loop(0, 4, tile, 0)
        copy_in([(st.at[8 * i : 8 * i + 8], ref) for i, ref in enumerate(out_refs)], sem)

    part = jax.ShapeDtypeStruct((8, 2, 4, SLICE, HD), jnp.float32)
    tiles = 4 * planes * HALF * 8 * 16 * HALF // 10
    return pl.pallas_call(
        kernel,
        out_shape=(part, part),
        in_specs=[SMEM] + [ANY] * (2 + n + (0 if held is None else 2)),
        out_specs=(ANY, ANY),
        scratch_shapes=[
            pltpu.VMEM((planes * 8, 2, 6, SLICE, HD), jnp.bfloat16),
            pltpu.VMEM((16, 2, 3, SLICE, HD), jnp.bfloat16),
            pltpu.VMEM((16, 2, 4, SLICE, HD), jnp.float32),
            pltpu.SemaphoreType.DMA,
        ],
        compiler_params=pltpu.CompilerParams(vmem_limit_bytes=28 * 2**20),
        cost_estimate=pl.CostEstimate(flops=tiles * 2560, bytes_accessed=8 * 2**20, transcendentals=tiles),
    )(sc, *queries, *pieces, *(held or ()))


def finish(sc, query, pieces, held):
    def kernel(sc, q_ref, p0, p1, p2, p3, own, other, out, kv, q, st_a, st_b, sem):
        pairs = [(q_ref, q), (own, st_a), (other, st_b)]
        pairs += [(ref, kv.at[4 * i : 4 * i + 4]) for i, ref in enumerate((p0, p1, p2, p3))]
        copy_in(pairs, sem)

        def tile(qt, _):
            info = query_tile(sc, q, FIRST[4], qt)
            at = INDEX + FIRST[4] + qt * QB
            state = join_states(gather_state(sc, st_a, at), gather_state(sc, st_b, at))
            low, high = sc[LOW + 2 * 6 + 4 + qt], sc[HIGH + 2 * 6 + 4 + qt]
            _, acc, acc_w = see(sc, kv, FIRST[2], info, state, low, high)
            inv = 1.0 / acc[:, 3 * HD :]
            primal = acc[:, :HD] * inv
            parts = [primal]
            for i in (1, 2):
                mine = slice((i - 1) * QT, i * QT)
                grad = acc[:, i * HD : (i + 1) * HD] + acc_w[mine, :HD] * SCALE
                parts.append(grad * inv - (acc_w[mine, HD:] * SCALE * inv) * primal)
            for i in range(QB):
                for t in range(3):
                    block = parts[t][i * HALF : i * HALF + HALF].reshape(2, SLICE, HD)
                    out[sc[at + i], :, t] = block.astype(jnp.bfloat16)
            return 0

        lax.fori_loop(0, 2, tile, 0)

    return pl.pallas_call(
        kernel,
        out_shape=jax.ShapeDtypeStruct((8, 2, 3, SLICE, HD), jnp.bfloat16),
        in_specs=[SMEM] + [ANY] * 7,
        out_specs=VMEM,
        scratch_shapes=[
            pltpu.VMEM((16, 2, 6, SLICE, HD), jnp.bfloat16),
            pltpu.VMEM((8, 2, 3, SLICE, HD), jnp.bfloat16),
            pltpu.VMEM((8, 2, 4, SLICE, HD), jnp.float32),
            pltpu.VMEM((8, 2, 4, SLICE, HD), jnp.float32),
            pltpu.SemaphoreType.DMA,
        ],
        compiler_params=pltpu.CompilerParams(vmem_limit_bytes=28 * 2**20),
    )(sc, query, *pieces, *held)


def hop(block, direction):
    return lax.ppermute(block, Z, [(i, (i + direction) % NZ) for i in range(NZ)])


def swap_cores(block):
    return lax.ppermute(block, "c", [(0, 1), (1, 0)])


def shards(query_set, key_set, value_set, block_order, documents):
    kv = lax.all_to_all(split_heads(key_set, value_set), XY, 0, 0)
    kv = kv.reshape(8, 2, 6, SLICE, HD)
    q = lax.all_to_all(split_heads(query_set), XY, 0, 0).reshape(8, 2, 3, SLICE, HD)
    pieces = {(half, 0): kv[4 * half : 4 * half + 4] for half in range(2)}
    ups = [pieces[0, 0], pieces[1, 0]]
    downs = [pieces[0, 0], pieces[1, 0]]
    for step in range(1, 5):
        for half in range(2):
            if step < 4 or half == 0:
                ups[half] = pieces[half, -step] = hop(ups[half], 1)
            if step < 4 or half == 1:
                downs[half] = pieces[half, step] = hop(downs[half], -1)
    sc = scalars(block_order, documents, *(lax.axis_index(a) for a in ("zh", "zl", "c")))
    queries = (q, swap_cores(q))
    state = attend(sc, queries, [pieces[half, o] for o in NEAR for half in range(2)], 0)
    own, other = attend(sc, queries, [pieces[half, o] for o in NEXT for half in range(2)], 1, state)
    far = [pieces[0, -4], pieces[1, 4]]
    done = finish(sc, q, [*far, *(swap_cores(p) for p in far)], (own, swap_cores(other)))
    done = lax.all_to_all(done.reshape(HEADS, 3, SLICE, HD), XY, 0, 0)
    return join_heads(done)


def solution(mesh):
    fine = Mesh(mesh.devices.reshape(SIZES), NAMES)
    rows = P(None, NAMES, None)
    return jax.shard_map(
        shards,
        mesh=fine,
        in_specs=(rows, rows, rows, P(), P()),
        out_specs=rows,
        check_vma=False,
    )
```

```python
import jax
import jax.numpy as jnp
from jax import lax
from jax.experimental import pallas as pl
from jax.experimental.pallas import tpu as pltpu
from jax.sharding import Mesh
from jax.sharding import PartitionSpec as P

HD = 128
HEADS = 16
BLOCK = 128
SLICE = 32
HALF = 2 * SLICE
Z = ("zh", "zl")
XY = ("y", "xh", "xl")
NAMES = ("zh", "y", "c", "xh", "xl", "zl")
SIZES = (4, 4, 2, 2, 2, 2)
NZ = 8
SCALE = 1.0 / HD**0.5
EXPONENT = SCALE * 1.4426950408889634
HIDDEN = -1e30
GRANT = 16 * 2**20
VMEM = pl.BlockSpec(memory_space=pltpu.VMEM)
SMEM = pl.BlockSpec(memory_space=pltpu.SMEM)
ANY = pl.BlockSpec(memory_space=pl.ANY)
NT = (((1,), (1,)), ((), ()))

NEAR = (-2, -1, 0, 1, 2)
NEXT = (-3, 3)
FAR = (4,)
FIRST = (0, 40, 56, 72, 88)
N_SLOTS = 96
QB, KB = 4, 8
QT, KT = QB * HALF, KB * HALF
INDEX, BASE, LOW, HIGH, STARTS = 0, 96, 192, 210, 228


def split_heads(*arrays):
    def kernel(*refs):
        out = refs[-1]
        for h in range(HEADS):
            for a, ref in enumerate(refs[:-1]):
                out[h, 3 * a : 3 * a + 3] = ref[:, :, h * HD : (h + 1) * HD]

    return pl.pallas_call(
        kernel,
        out_shape=jax.ShapeDtypeStruct((HEADS, 3 * len(arrays), SLICE, HD), jnp.bfloat16),
        in_specs=[VMEM] * len(arrays),
        out_specs=VMEM,
    )(*arrays)


def join_heads(parts):
    def kernel(ref, out):
        for h in range(HEADS):
            out[:, :, h * HD : (h + 1) * HD] = ref[h]

    return pl.pallas_call(
        kernel,
        out_shape=jax.ShapeDtypeStruct((3, SLICE, HEADS * HD), jnp.bfloat16),
        in_specs=[VMEM],
        out_specs=VMEM,
    )(parts)


def scalars(order, documents, zh, zl, c):
    i32 = jnp.int32
    z = zh * 2 + zl
    rows = [(o, 0, 0) for o in NEAR]
    rows += [(o, 0, 1) for o in NEXT]
    rows += [(o, other, 2) for other in range(2) for o in FAR]
    rows += [(0, 0, 3), (0, 1, 3), (0, 0, 4)]
    offsets, cores, sets = (jnp.array(v, i32) for v in zip(*rows, strict=True))
    begins = jnp.array([FIRST[r[2]] // 8 for r in rows], i32)
    planes = lax.rem(z + offsets + NZ, NZ)
    table = order.reshape(4, 4, 2, 2).transpose(0, 2, 1, 3).reshape(8, 8)
    line = planes // 2 * 2 + lax.rem(cores + c, 2)
    hit = line[:, None] == jnp.arange(8, dtype=i32)[None, :]
    pos = jnp.sum(jnp.where(hit[:, :, None], table[None], 0), axis=1)
    code = (sets[:, None] * 4096 + pos * 2 + lax.rem(planes, 2)[:, None]).reshape(-1)
    payload = ((jnp.arange(len(rows), dtype=i32) - begins)[:, None] * 8 + jnp.arange(8, dtype=i32)[None, :]).reshape(-1)
    rank = jnp.sum((code[None, :] < code[:, None]).astype(i32), axis=1)
    slot = jnp.arange(N_SLOTS, dtype=i32)
    hits = rank[None, :] == slot[:, None]
    index = jnp.sum(jnp.where(hits, payload[None, :], 0), axis=1)
    low_bits = code % 4096
    base_of = low_bits // 2 * BLOCK + low_bits % 2 * SLICE
    base = jnp.sum(jnp.where(hits, base_of[None, :], 0), axis=1)
    starts = jnp.sum((documents[None, :] < jnp.arange(1, 4, dtype=i32)[:, None]).astype(i32), axis=1)
    first = base[FIRST[3] :: QB]
    last = base[FIRST[3] + QB - 1 :: QB] + BLOCK - SLICE
    begin = jnp.max(jnp.where(starts[None, :] <= first[:, None], starts[None, :], 0), axis=1)
    set_of = code // 4096
    member = set_of[None, None, :] == jnp.arange(3, dtype=i32)[:, None, None]
    before = base_of[None, None, :] + BLOCK - SLICE <= begin[None, :, None]
    upto = base_of[None, None, :] < last[None, :, None]
    low = jnp.sum((member & before).astype(i32), axis=2) // KB
    high = (jnp.sum((member & upto).astype(i32), axis=2) + KB - 1) // KB
    return jnp.concatenate([index, base, low.reshape(-1), high.reshape(-1), starts])


def lookup(sc, at, count, position, size):
    out = sc[at]
    for i in range(1, count):
        out = jnp.where(position >= i * size, sc[at + i], out)
    return out


def within(position):
    return lax.rem(position, HALF) // SLICE * HALF + lax.rem(position, SLICE)


def gathered(sc, ref, at, count, t):
    return jnp.concatenate([ref[sc[at + i], :, t].reshape(HALF, HD) for i in range(count)], 0)


def query_tile(sc, q, first, tile):
    at = first + tile * QB
    q0, q1, q2 = (gathered(sc, q, INDEX + at, QB, t) for t in range(3))
    row = lax.broadcasted_iota(jnp.int32, (QT, 1), 0)
    qpos = lookup(sc, BASE + at, QB, row, HALF) + within(row)
    start = jnp.zeros_like(qpos)
    for d in range(3):
        start = jnp.where(qpos >= sc[STARTS + d], sc[STARTS + d], start)
    return q0, jnp.concatenate([q1, q0], 1), jnp.concatenate([q2, q0], 1), qpos, start


def see(sc, k, v, first, queries, state, low, high):
    q0, q10, q20, qpos, start = queries
    col = lax.broadcasted_iota(jnp.int32, (1, KT), 1)
    ones = jnp.ones((KT, HD), jnp.bfloat16)

    def step(kt, state):
        top, acc, acc_w = state
        at = first + kt * KB
        k0, k1, k2 = (gathered(sc, k, INDEX + at, KB, t) for t in range(3))
        v0, v1, v2 = (gathered(sc, v, INDEX + at, KB, t) for t in range(3))
        kpos = lookup(sc, BASE + at, KB, col, HALF) + within(col)
        s = lax.dot_general(q0, k0, NT, preferred_element_type=jnp.float32)
        d1 = lax.dot_general(q10, jnp.concatenate([k0, k1], 1), NT, preferred_element_type=jnp.float32)
        d2 = lax.dot_general(q20, jnp.concatenate([k0, k2], 1), NT, preferred_element_type=jnp.float32)
        s = jnp.where((kpos <= qpos) & (kpos >= start), s, HIDDEN)
        peak = jnp.maximum(jnp.maximum(s[:, :HD], s[:, HD : 2 * HD]), jnp.maximum(s[:, 2 * HD : 3 * HD], s[:, 3 * HD :]))
        new = jnp.maximum(top, jnp.max(peak, axis=1, keepdims=True))
        shrink = jnp.exp2((top - new) * EXPONENT)
        shift = jnp.where(new < 0.5 * HIDDEN, 0.0, new)[:, :1]
        e = jnp.exp2((s - shift) * EXPONENT)
        w = jnp.concatenate([(e * d1).astype(jnp.bfloat16), (e * d2).astype(jnp.bfloat16)], 0)
        shrink4 = jnp.concatenate([shrink] * 4, 1)
        shrink2 = shrink4[:, : 2 * HD]
        acc = acc * shrink4 + jnp.dot(
            e.astype(jnp.bfloat16), jnp.concatenate([v0, v1, v2, ones], 1), preferred_element_type=jnp.float32
        )
        acc_w = acc_w * jnp.concatenate([shrink2, shrink2], 0) + jnp.dot(
            w, jnp.concatenate([v0, ones], 1), preferred_element_type=jnp.float32
        )
        return new, acc, acc_w

    return lax.fori_loop(low, high, step, state)


def fresh():
    return (
        jnp.full((QT, HD), HIDDEN, jnp.float32),
        jnp.zeros((QT, 4 * HD), jnp.float32),
        jnp.zeros((2 * QT, 2 * HD), jnp.float32),
    )


def pack_state(state):
    top, acc, acc_w = state
    total, c1, c2 = acc[:, 3 * HD :], acc_w[:QT, HD:] * SCALE, acc_w[QT:, HD:] * SCALE
    lane = lax.broadcasted_iota(jnp.int32, (QT, HD), 1)
    stats = jnp.where(lane == 0, top, jnp.where(lane == 1, total, jnp.where(lane == 2, c1, c2)))
    return (
        acc[:, :HD],
        acc[:, HD : 2 * HD] + acc_w[:QT, :HD] * SCALE,
        acc[:, 2 * HD : 3 * HD] + acc_w[QT:, :HD] * SCALE,
        stats,
    )


def unpack_state(parts):
    a, g1, g2, stats = parts
    top, total, c1, c2 = (jnp.broadcast_to(stats[:, i : i + 1], (QT, HD)) for i in range(4))
    zero = jnp.zeros((QT, HD), jnp.float32)
    acc = jnp.concatenate([a, g1, g2, total], 1)
    c = jnp.concatenate([c1, c2], 0) * (1.0 / SCALE)
    return top, acc, jnp.concatenate([jnp.concatenate([zero, zero], 0), c], 1)


def join_states(one, two):
    top = jnp.maximum(one[0], two[0])
    f, g = (jnp.exp2((t - top) * EXPONENT) for t in (one[0], two[0]))
    f4, g4 = (jnp.concatenate([v] * 4, 1) for v in (f, g))
    f2, g2 = (jnp.concatenate([v[:, : 2 * HD]] * 2, 0) for v in (f4, g4))
    return top, one[1] * f4 + two[1] * g4, one[2] * f2 + two[2] * g2


def gather_state(sc, ref, at):
    return unpack_state([gathered(sc, ref, at, QB, t) for t in range(4)])


def copy_in(pairs, sem):
    copies = [pltpu.make_async_copy(src, dst, sem) for src, dst in pairs]
    for copy in copies:
        copy.start()
    for copy in copies:
        copy.wait()


def kernel_state(rows):
    return pltpu.VMEM((rows, 2, 4, SLICE, HD), jnp.float32)


def key_scratch(planes):
    return [pltpu.VMEM((planes * 8, 2, 3, SLICE, HD), jnp.bfloat16) for _ in range(2)]


def plane_copies(refs, k, v):
    n = len(refs) // 2
    return [(ref, (k, v)[i // n].at[pl.ds(i % n * 8, 8)]) for i, ref in enumerate(refs)]


def estimate(queries, keys):
    pairs = queries * keys // 4
    return pl.CostEstimate(flops=pairs * 2560, bytes_accessed=8 * 2**20, transcendentals=pairs)


def attend(sc, queries, planes, key_set, held=()):
    n = len(planes)

    def kernel(sc, q_own, q_other, *refs):
        kv_refs, refs = refs[:n], refs[n:]
        held_refs, refs = refs[: len(held)], refs[len(held) :]
        out_refs, (k, v, q, st, sem) = refs[:2], refs[2:]
        before = [(ref, st.at[8 * i : 8 * i + 8]) for i, ref in enumerate(held_refs)]
        copy_in([(q_own, q.at[0:8]), (q_other, q.at[8:16]), *before, *plane_copies(kv_refs, k, v)], sem)

        def tile(qt, _):
            at = INDEX + FIRST[3] + qt * QB
            low, high = sc[LOW + key_set * 6 + qt], sc[HIGH + key_set * 6 + qt]

            def work():
                info = query_tile(sc, q, FIRST[3], qt)
                state = gather_state(sc, st, at) if held else fresh()
                parts = pack_state(see(sc, k, v, FIRST[key_set], info, state, low, high))
                for i in range(QB):
                    for t in range(4):
                        st[sc[at + i], :, t] = parts[t][i * HALF : i * HALF + HALF].reshape(2, SLICE, HD)

            if held:
                pl.when(high > low)(work)
            else:
                work()
            return 0

        lax.fori_loop(0, 4, tile, 0)
        copy_in([(st.at[8 * i : 8 * i + 8], ref) for i, ref in enumerate(out_refs)], sem)

    part = jax.ShapeDtypeStruct((8, 2, 4, SLICE, HD), jnp.float32)
    return pl.pallas_call(
        kernel,
        out_shape=(part, part),
        in_specs=[SMEM] + [ANY] * (2 + n + len(held)),
        out_specs=(ANY, ANY),
        scratch_shapes=[
            *key_scratch(n // 2),
            pltpu.VMEM((16, 2, 3, SLICE, HD), jnp.bfloat16),
            kernel_state(16),
            pltpu.SemaphoreType.DMA,
        ],
        compiler_params=pltpu.CompilerParams(vmem_limit_bytes=GRANT),
        cost_estimate=estimate(1024, n // 2 * 512),
    )(sc, *queries, *planes, *held)


def finish(sc, query, planes, held):
    n = len(planes)

    def kernel(sc, q_ref, *refs):
        kv_refs, held_refs = refs[:n], refs[n : n + 2]
        out, k, v, q, one, two, sem = refs[n + 2 :]
        copy_in([(q_ref, q), (held_refs[0], one), (held_refs[1], two), *plane_copies(kv_refs, k, v)], sem)

        def tile(qt, _):
            at = INDEX + FIRST[4] + qt * QB
            info = query_tile(sc, q, FIRST[4], qt)
            state = join_states(gather_state(sc, one, at), gather_state(sc, two, at))
            low, high = sc[LOW + 2 * 6 + 4 + qt], sc[HIGH + 2 * 6 + 4 + qt]
            parts = results(see(sc, k, v, FIRST[2], info, state, low, high))
            for i in range(QB):
                for t, part in enumerate(parts):
                    block = part[i * HALF : i * HALF + HALF].reshape(2, SLICE, HD)
                    out[sc[at + i], :, t] = block.astype(jnp.bfloat16)
            return 0

        lax.fori_loop(0, 2, tile, 0)

    return pl.pallas_call(
        kernel,
        out_shape=jax.ShapeDtypeStruct((8, 2, 3, SLICE, HD), jnp.bfloat16),
        in_specs=[SMEM] + [ANY] * (3 + n),
        out_specs=VMEM,
        scratch_shapes=[
            *key_scratch(n // 2),
            pltpu.VMEM((8, 2, 3, SLICE, HD), jnp.bfloat16),
            kernel_state(8),
            kernel_state(8),
            pltpu.SemaphoreType.DMA,
        ],
        compiler_params=pltpu.CompilerParams(vmem_limit_bytes=GRANT),
        cost_estimate=estimate(512, n // 2 * 512),
    )(sc, query, *planes, *held)


def results(state):
    _, acc, acc_w = state
    inv = 1.0 / acc[:, 3 * HD :]
    primal = acc[:, :HD] * inv
    parts = [primal]
    for i in (1, 2):
        mine = slice((i - 1) * QT, i * QT)
        grad = acc[:, i * HD : (i + 1) * HD] + acc_w[mine, :HD] * SCALE
        parts.append(grad * inv - (acc_w[mine, HD:] * SCALE * inv) * primal)
    return parts


def hop(block, direction):
    return lax.ppermute(block, Z, [(i, (i + direction) % NZ) for i in range(NZ)])


def swap_cores(block):
    return lax.ppermute(block, "c", [(0, 1), (1, 0)])


def to_heads(array):
    return lax.all_to_all(split_heads(array), XY, 0, 0).reshape(8, 2, 3, SLICE, HD)


def shards(query_set, key_set, value_set, block_order, documents):
    planes = {0: [to_heads(key_set), to_heads(value_set)]}
    for step in range(1, 4):
        planes[-step] = [hop(p, 1) for p in planes[1 - step]]
        planes[step] = [hop(p, -1) for p in planes[step - 1]]
    query_set, _ = lax.optimization_barrier((query_set, planes[1][0]))
    q = to_heads(query_set)
    sc = scalars(block_order, documents, *(lax.axis_index(a) for a in ("zh", "zl", "c")))
    queries = (q, swap_cores(q))
    state = attend(sc, queries, [planes[o][t] for t in range(2) for o in NEAR], 0)
    state, planes[-3][0], planes[3][1] = lax.optimization_barrier((state, planes[-3][0], planes[3][1]))
    far = [hop(planes[-3][0], 1), hop(planes[3][1], -1)]
    own, other = attend(sc, queries, [planes[o][t] for t in range(2) for o in NEXT], 1, state)
    own, other, far = lax.optimization_barrier((own, other, far))
    far = [p for f in far for p in (f, swap_cores(f))]
    done = finish(sc, q, far, (own, swap_cores(other)))
    done = lax.all_to_all(done.reshape(HEADS, 3, SLICE, HD), XY, 0, 0)
    return join_heads(done)


def solution(mesh):
    fine = Mesh(mesh.devices.reshape(SIZES), NAMES)
    rows = P(None, NAMES, None)
    return jax.shard_map(
        shards,
        mesh=fine,
        in_specs=(rows, rows, rows, P(), P()),
        out_specs=rows,
        check_vma=False,
    )
```

```python
import jax
import jax.numpy as jnp
from jax import lax
from jax.experimental import pallas as pl
from jax.experimental.pallas import tpu as pltpu
from jax.sharding import Mesh
from jax.sharding import PartitionSpec as P

HD = 128
HEADS = 16
BLOCK = 128
SLICE = 32
HALF = 2 * SLICE
Z = ("zh", "zl")
XY = ("y", "xh", "xl")
NAMES = ("zh", "y", "c", "xh", "xl", "zl")
SIZES = (4, 4, 2, 2, 2, 2)
NZ = 8
SCALE = 1.0 / HD**0.5
EXPONENT = SCALE * 1.4426950408889634
HIDDEN = -1e30
GRANT = 16 * 2**20
VMEM = pl.BlockSpec(memory_space=pltpu.VMEM)
SMEM = pl.BlockSpec(memory_space=pltpu.SMEM)
ANY = pl.BlockSpec(memory_space=pl.ANY)
NT = (((1,), (1,)), ((), ()))

NEAR = (-2, -1, 0, 1, 2)
NEXT = (-3, 3)
FAR = (4,)
FIRST = (0, 40, 56, 72, 88)
N_SLOTS = 96
QB, KB = 4, 8
QT, KT = QB * HALF, KB * HALF
INDEX, BASE, LOW, HIGH, STARTS = 0, 96, 192, 210, 228


def split_heads(*arrays):
    def kernel(*refs):
        out = refs[-1]
        for h in range(HEADS):
            for a, ref in enumerate(refs[:-1]):
                out[h, 3 * a : 3 * a + 3] = ref[:, :, h * HD : (h + 1) * HD]

    return pl.pallas_call(
        kernel,
        out_shape=jax.ShapeDtypeStruct((HEADS, 3 * len(arrays), SLICE, HD), jnp.bfloat16),
        in_specs=[VMEM] * len(arrays),
        out_specs=VMEM,
    )(*arrays)


def join_heads(parts):
    def kernel(ref, out):
        for h in range(HEADS):
            out[:, :, h * HD : (h + 1) * HD] = ref[h]

    return pl.pallas_call(
        kernel,
        out_shape=jax.ShapeDtypeStruct((3, SLICE, HEADS * HD), jnp.bfloat16),
        in_specs=[VMEM],
        out_specs=VMEM,
    )(parts)


def scalars(order, documents, zh, zl, c):
    i32 = jnp.int32
    z = zh * 2 + zl
    rows = [(o, 0, 0) for o in NEAR]
    rows += [(o, 0, 1) for o in NEXT]
    rows += [(o, other, 2) for other in range(2) for o in FAR]
    rows += [(0, 0, 3), (0, 1, 3), (0, 0, 4)]
    offsets, cores, sets = (jnp.array(v, i32) for v in zip(*rows, strict=True))
    begins = jnp.array([FIRST[r[2]] // 8 for r in rows], i32)
    planes = lax.rem(z + offsets + NZ, NZ)
    table = order.reshape(4, 4, 2, 2).transpose(0, 2, 1, 3).reshape(8, 8)
    line = planes // 2 * 2 + lax.rem(cores + c, 2)
    hit = line[:, None] == jnp.arange(8, dtype=i32)[None, :]
    pos = jnp.sum(jnp.where(hit[:, :, None], table[None], 0), axis=1)
    code = (sets[:, None] * 4096 + pos * 2 + lax.rem(planes, 2)[:, None]).reshape(-1)
    payload = ((jnp.arange(len(rows), dtype=i32) - begins)[:, None] * 8 + jnp.arange(8, dtype=i32)[None, :]).reshape(-1)
    rank = jnp.sum((code[None, :] < code[:, None]).astype(i32), axis=1)
    slot = jnp.arange(N_SLOTS, dtype=i32)
    hits = rank[None, :] == slot[:, None]
    index = jnp.sum(jnp.where(hits, payload[None, :], 0), axis=1)
    low_bits = code % 4096
    base_of = low_bits // 2 * BLOCK + low_bits % 2 * SLICE
    base = jnp.sum(jnp.where(hits, base_of[None, :], 0), axis=1)
    starts = jnp.sum((documents[None, :] < jnp.arange(1, 4, dtype=i32)[:, None]).astype(i32), axis=1)
    first = base[FIRST[3] :: QB]
    last = base[FIRST[3] + QB - 1 :: QB] + BLOCK - SLICE
    begin = jnp.max(jnp.where(starts[None, :] <= first[:, None], starts[None, :], 0), axis=1)
    set_of = code // 4096
    member = set_of[None, None, :] == jnp.arange(3, dtype=i32)[:, None, None]
    before = base_of[None, None, :] + BLOCK - SLICE <= begin[None, :, None]
    upto = base_of[None, None, :] < last[None, :, None]
    low = jnp.sum((member & before).astype(i32), axis=2) // KB
    high = (jnp.sum((member & upto).astype(i32), axis=2) + KB - 1) // KB
    return jnp.concatenate([index, base, low.reshape(-1), high.reshape(-1), starts])


def lookup(sc, at, count, position, size):
    out = sc[at]
    for i in range(1, count):
        out = jnp.where(position >= i * size, sc[at + i], out)
    return out


def within(position):
    return lax.rem(position, HALF) // SLICE * HALF + lax.rem(position, SLICE)


def gathered(sc, ref, at, count, t):
    return jnp.concatenate([ref[sc[at + i], :, t].reshape(HALF, HD) for i in range(count)], 0)


def query_tile(sc, q, first, tile):
    at = first + tile * QB
    q0, q1, q2 = (gathered(sc, q, INDEX + at, QB, t) for t in range(3))
    row = lax.broadcasted_iota(jnp.int32, (QT, 1), 0)
    qpos = lookup(sc, BASE + at, QB, row, HALF) + within(row)
    start = jnp.zeros_like(qpos)
    for d in range(3):
        start = jnp.where(qpos >= sc[STARTS + d], sc[STARTS + d], start)
    return q0, jnp.concatenate([q1, q0], 1), jnp.concatenate([q2, q0], 1), qpos, start


def see(sc, kv, first, queries, state, low, high):
    q0, q10, q20, qpos, start = queries
    col = lax.broadcasted_iota(jnp.int32, (1, KT), 1)
    ones = jnp.ones((KT, HD), jnp.bfloat16)

    def step(kt, state):
        top, acc, acc_w = state
        at = first + kt * KB
        k0, k1, k2, v0, v1, v2 = (gathered(sc, kv, INDEX + at, KB, t) for t in range(6))
        kpos = lookup(sc, BASE + at, KB, col, HALF) + within(col)
        s = lax.dot_general(q0, k0, NT, preferred_element_type=jnp.float32)
        d1 = lax.dot_general(q10, jnp.concatenate([k0, k1], 1), NT, preferred_element_type=jnp.float32)
        d2 = lax.dot_general(q20, jnp.concatenate([k0, k2], 1), NT, preferred_element_type=jnp.float32)
        s = jnp.where((kpos <= qpos) & (kpos >= start), s, HIDDEN)
        peak = jnp.maximum(jnp.maximum(s[:, :HD], s[:, HD : 2 * HD]), jnp.maximum(s[:, 2 * HD : 3 * HD], s[:, 3 * HD :]))
        new = jnp.maximum(top, jnp.max(peak, axis=1, keepdims=True))
        shrink = jnp.exp2((top - new) * EXPONENT)
        shift = jnp.where(new < 0.5 * HIDDEN, 0.0, new)[:, :1]
        e = jnp.exp2((s - shift) * EXPONENT)
        w = jnp.concatenate([(e * d1).astype(jnp.bfloat16), (e * d2).astype(jnp.bfloat16)], 0)
        shrink4 = jnp.concatenate([shrink] * 4, 1)
        shrink2 = shrink4[:, : 2 * HD]
        acc = acc * shrink4 + jnp.dot(
            e.astype(jnp.bfloat16), jnp.concatenate([v0, v1, v2, ones], 1), preferred_element_type=jnp.float32
        )
        acc_w = acc_w * jnp.concatenate([shrink2, shrink2], 0) + jnp.dot(
            w, jnp.concatenate([v0, ones], 1), preferred_element_type=jnp.float32
        )
        return new, acc, acc_w

    return lax.fori_loop(low, high, step, state)


def fresh():
    return (
        jnp.full((QT, HD), HIDDEN, jnp.float32),
        jnp.zeros((QT, 4 * HD), jnp.float32),
        jnp.zeros((2 * QT, 2 * HD), jnp.float32),
    )


def pack_state(state):
    top, acc, acc_w = state
    total, c1, c2 = acc[:, 3 * HD :], acc_w[:QT, HD:] * SCALE, acc_w[QT:, HD:] * SCALE
    lane = lax.broadcasted_iota(jnp.int32, (QT, HD), 1)
    stats = jnp.where(lane == 0, top, jnp.where(lane == 1, total, jnp.where(lane == 2, c1, c2)))
    return (
        acc[:, :HD],
        acc[:, HD : 2 * HD] + acc_w[:QT, :HD] * SCALE,
        acc[:, 2 * HD : 3 * HD] + acc_w[QT:, :HD] * SCALE,
        stats,
    )


def unpack_state(parts):
    a, g1, g2, stats = parts
    top, total, c1, c2 = (jnp.broadcast_to(stats[:, i : i + 1], (QT, HD)) for i in range(4))
    zero = jnp.zeros((QT, HD), jnp.float32)
    acc = jnp.concatenate([a, g1, g2, total], 1)
    c = jnp.concatenate([c1, c2], 0) * (1.0 / SCALE)
    return top, acc, jnp.concatenate([jnp.concatenate([zero, zero], 0), c], 1)


def join_states(one, two):
    top = jnp.maximum(one[0], two[0])
    f, g = (jnp.exp2((t - top) * EXPONENT) for t in (one[0], two[0]))
    f4, g4 = (jnp.concatenate([v] * 4, 1) for v in (f, g))
    f2, g2 = (jnp.concatenate([v[:, : 2 * HD]] * 2, 0) for v in (f4, g4))
    return top, one[1] * f4 + two[1] * g4, one[2] * f2 + two[2] * g2


def gather_state(sc, ref, at):
    return unpack_state([gathered(sc, ref, at, QB, t) for t in range(4)])


def copy_in(pairs, sem):
    copies = [pltpu.make_async_copy(src, dst, sem) for src, dst in pairs]
    for copy in copies:
        copy.start()
    for copy in copies:
        copy.wait()


def kernel_state(rows):
    return pltpu.VMEM((rows, 2, 4, SLICE, HD), jnp.float32)


def key_scratch(planes):
    return pltpu.VMEM((planes * 8, 2, 6, SLICE, HD), jnp.bfloat16)


def plane_copies(refs, kv):
    return [(ref, kv.at[4 * i : 4 * i + 4]) for i, ref in enumerate(refs)]


def estimate(queries, keys):
    pairs = queries * keys // 4
    return pl.CostEstimate(flops=pairs * 2560, bytes_accessed=8 * 2**20, transcendentals=pairs)


def attend(sc, queries, planes, key_set, held=()):
    n = len(planes)

    def kernel(sc, q_own, q_other, *refs):
        kv_refs, refs = refs[:n], refs[n:]
        held_refs, refs = refs[: len(held)], refs[len(held) :]
        out_refs, (kv, q, st, sem) = refs[:2], refs[2:]
        before = [(ref, st.at[8 * i : 8 * i + 8]) for i, ref in enumerate(held_refs)]
        copy_in([(q_own, q.at[0:8]), (q_other, q.at[8:16]), *before, *plane_copies(kv_refs, kv)], sem)

        def tile(qt, _):
            at = INDEX + FIRST[3] + qt * QB
            low, high = sc[LOW + key_set * 6 + qt], sc[HIGH + key_set * 6 + qt]

            def work():
                info = query_tile(sc, q, FIRST[3], qt)
                state = gather_state(sc, st, at) if held else fresh()
                parts = pack_state(see(sc, kv, FIRST[key_set], info, state, low, high))
                for i in range(QB):
                    for t in range(4):
                        st[sc[at + i], :, t] = parts[t][i * HALF : i * HALF + HALF].reshape(2, SLICE, HD)

            if held:
                pl.when(high > low)(work)
            else:
                work()
            return 0

        lax.fori_loop(0, 4, tile, 0)
        copy_in([(st.at[8 * i : 8 * i + 8], ref) for i, ref in enumerate(out_refs)], sem)

    part = jax.ShapeDtypeStruct((8, 2, 4, SLICE, HD), jnp.float32)
    return pl.pallas_call(
        kernel,
        out_shape=(part, part),
        in_specs=[SMEM] + [ANY] * (2 + n + len(held)),
        out_specs=(ANY, ANY),
        scratch_shapes=[
            key_scratch(n // 2),
            pltpu.VMEM((16, 2, 3, SLICE, HD), jnp.bfloat16),
            kernel_state(16),
            pltpu.SemaphoreType.DMA,
        ],
        compiler_params=pltpu.CompilerParams(vmem_limit_bytes=GRANT),
        cost_estimate=estimate(1024, n // 2 * 512),
    )(sc, *queries, *planes, *held)


def finish(sc, query, planes, held):
    n = len(planes)

    def kernel(sc, q_ref, *refs):
        kv_refs, held_refs = refs[:n], refs[n : n + 2]
        out, kv, q, one, two, sem = refs[n + 2 :]
        copy_in([(q_ref, q), (held_refs[0], one), (held_refs[1], two), *plane_copies(kv_refs, kv)], sem)

        def tile(qt, _):
            at = INDEX + FIRST[4] + qt * QB
            info = query_tile(sc, q, FIRST[4], qt)
            state = join_states(gather_state(sc, one, at), gather_state(sc, two, at))
            low, high = sc[LOW + 2 * 6 + 4 + qt], sc[HIGH + 2 * 6 + 4 + qt]
            parts = results(see(sc, kv, FIRST[2], info, state, low, high))
            for i in range(QB):
                for t, part in enumerate(parts):
                    block = part[i * HALF : i * HALF + HALF].reshape(2, SLICE, HD)
                    out[sc[at + i], :, t] = block.astype(jnp.bfloat16)
            return 0

        lax.fori_loop(0, 2, tile, 0)

    return pl.pallas_call(
        kernel,
        out_shape=jax.ShapeDtypeStruct((8, 2, 3, SLICE, HD), jnp.bfloat16),
        in_specs=[SMEM] + [ANY] * (3 + n),
        out_specs=VMEM,
        scratch_shapes=[
            key_scratch(n // 2),
            pltpu.VMEM((8, 2, 3, SLICE, HD), jnp.bfloat16),
            kernel_state(8),
            kernel_state(8),
            pltpu.SemaphoreType.DMA,
        ],
        compiler_params=pltpu.CompilerParams(vmem_limit_bytes=GRANT),
        cost_estimate=estimate(512, n // 2 * 512),
    )(sc, query, *planes, *held)


def results(state):
    _, acc, acc_w = state
    inv = 1.0 / acc[:, 3 * HD :]
    primal = acc[:, :HD] * inv
    parts = [primal]
    for i in (1, 2):
        mine = slice((i - 1) * QT, i * QT)
        grad = acc[:, i * HD : (i + 1) * HD] + acc_w[mine, :HD] * SCALE
        parts.append(grad * inv - (acc_w[mine, HD:] * SCALE * inv) * primal)
    return parts


def hop(block, direction):
    return lax.ppermute(block, Z, [(i, (i + direction) % NZ) for i in range(NZ)])


def swap_cores(block):
    return lax.ppermute(block, "c", [(0, 1), (1, 0)])


def shards(query_set, key_set, value_set, block_order, documents):
    kv = lax.all_to_all(split_heads(key_set, value_set), XY, 0, 0).reshape(8, 2, 6, SLICE, HD)
    sc = scalars(block_order, documents, *(lax.axis_index(a) for a in ("zh", "zl", "c")))
    kv, q, sc = lax.optimization_barrier((kv, split_heads(query_set), sc))
    q = lax.all_to_all(q, XY, 0, 0).reshape(8, 2, 3, SLICE, HD)
    planes = {0: [kv[:4], kv[4:]]}
    for step in range(1, 4):
        planes[-step] = [hop(p, 1) for p in planes[1 - step]]
        planes[step] = [hop(p, -1) for p in planes[step - 1]]
    queries = (q, swap_cores(q))
    state = attend(sc, queries, [p for o in NEAR for p in planes[o]], 0)
    state, planes[-3][0], planes[3][1] = lax.optimization_barrier((state, planes[-3][0], planes[3][1]))
    far = [hop(planes[-3][0], 1), hop(planes[3][1], -1)]
    own, other = attend(sc, queries, [p for o in NEXT for p in planes[o]], 1, state)
    own, other, far = lax.optimization_barrier((own, other, far))
    done = finish(sc, q, [*far, *map(swap_cores, far)], (own, swap_cores(other)))
    done = lax.all_to_all(done.reshape(HEADS, 3, SLICE, HD), XY, 0, 0)
    return join_heads(done)


def solution(mesh):
    fine = Mesh(mesh.devices.reshape(SIZES), NAMES)
    rows = P(None, NAMES, None)
    return jax.shard_map(
        shards,
        mesh=fine,
        in_specs=(rows, rows, rows, P(), P()),
        out_specs=rows,
        check_vma=False,
    )
```

```python
import functools

import jax
import jax.numpy as jnp
from jax import lax
from jax.experimental import pallas as pl
from jax.experimental.pallas import tpu as pltpu
from jax.sharding import Mesh
from jax.sharding import PartitionSpec as P

HD = 128
HEADS = 16
BLOCK = 128
SLICE = 32
HALF = 2 * SLICE
Z = ("zh", "zl")
XY = ("y", "xh", "xl")
NAMES = ("zh", "y", "c", "xh", "xl", "zl")
SIZES = (4, 4, 2, 2, 2, 2)
NZ = 8
SCALE = 1.0 / HD**0.5
EXPONENT = SCALE * 1.4426950408889634
HIDDEN = -1e30
GRANT = 16 * 2**20
VMEM = pl.BlockSpec(memory_space=pltpu.VMEM)
SMEM = pl.BlockSpec(memory_space=pltpu.SMEM)
ANY = pl.BlockSpec(memory_space=pl.ANY)
NT = (((1,), (1,)), ((), ()))

SETS = ((-1, 0, 1), (-2, 2), (-3, 3), (4,))
LAST = 3
ALL, OWN = 4, 5
FIRST = (0, 24, 40, 56, 72, 88)
N_SLOTS = 96
QB, KB = 4, 8
QT, KT = QB * HALF, KB * HALF
INDEX, BASE, LOW, HIGH, STARTS = 0, 96, 192, 216, 240


def split_heads(*arrays):
    def kernel(*refs):
        out = refs[-1]
        for h in range(HEADS):
            for a, ref in enumerate(refs[:-1]):
                out[h, 3 * a : 3 * a + 3] = ref[:, :, h * HD : (h + 1) * HD]

    return pl.pallas_call(
        kernel,
        out_shape=jax.ShapeDtypeStruct((HEADS, 3 * len(arrays), SLICE, HD), jnp.bfloat16),
        in_specs=[VMEM] * len(arrays),
        out_specs=VMEM,
    )(*arrays)


def join_heads(parts):
    def kernel(ref, out):
        for h in range(HEADS):
            out[:, :, h * HD : (h + 1) * HD] = ref[h]

    return pl.pallas_call(
        kernel,
        out_shape=jax.ShapeDtypeStruct((3, SLICE, HEADS * HD), jnp.bfloat16),
        in_specs=[VMEM],
        out_specs=VMEM,
    )(parts)


def scalars(order, documents, zh, zl, c):
    i32 = jnp.int32
    z = zh * 2 + zl
    rows = [(o, 0, i) for i in range(LAST) for o in SETS[i]]
    rows += [(o, other, LAST) for other in range(2) for o in SETS[LAST]]
    rows += [(0, 0, ALL), (0, 1, ALL), (0, 0, OWN)]
    offsets, cores, sets = (jnp.array(v, i32) for v in zip(*rows, strict=True))
    begins = jnp.array([FIRST[r[2]] // 8 for r in rows], i32)
    planes = lax.rem(z + offsets + NZ, NZ)
    table = order.reshape(4, 4, 2, 2).transpose(0, 2, 1, 3).reshape(8, 8)
    line = planes // 2 * 2 + lax.rem(cores + c, 2)
    hit = line[:, None] == jnp.arange(8, dtype=i32)[None, :]
    pos = jnp.sum(jnp.where(hit[:, :, None], table[None], 0), axis=1)
    code = (sets[:, None] * 4096 + pos * 2 + lax.rem(planes, 2)[:, None]).reshape(-1)
    payload = ((jnp.arange(len(rows), dtype=i32) - begins)[:, None] * 8 + jnp.arange(8, dtype=i32)[None, :]).reshape(-1)
    rank = jnp.sum((code[None, :] < code[:, None]).astype(i32), axis=1)
    slot = jnp.arange(N_SLOTS, dtype=i32)
    hits = rank[None, :] == slot[:, None]
    index = jnp.sum(jnp.where(hits, payload[None, :], 0), axis=1)
    low_bits = code % 4096
    base_of = low_bits // 2 * BLOCK + low_bits % 2 * SLICE
    base = jnp.sum(jnp.where(hits, base_of[None, :], 0), axis=1)
    starts = jnp.sum((documents[None, :] < jnp.arange(1, 4, dtype=i32)[:, None]).astype(i32), axis=1)
    first = base[FIRST[ALL] :: QB]
    last = base[FIRST[ALL] + QB - 1 :: QB] + BLOCK - SLICE
    begin = jnp.max(jnp.where(starts[None, :] <= first[:, None], starts[None, :], 0), axis=1)
    set_of = code // 4096
    member = set_of[None, None, :] == jnp.arange(len(SETS), dtype=i32)[:, None, None]
    before = base_of[None, None, :] + BLOCK - SLICE <= begin[None, :, None]
    upto = base_of[None, None, :] < last[None, :, None]
    low = jnp.sum((member & before).astype(i32), axis=2) // KB
    high = (jnp.sum((member & upto).astype(i32), axis=2) + KB - 1) // KB
    return jnp.concatenate([index, base, low.reshape(-1), high.reshape(-1), starts])


def lookup(sc, at, count, position, size):
    out = sc[at]
    for i in range(1, count):
        out = jnp.where(position >= i * size, sc[at + i], out)
    return out


def within(position):
    return (position & SLICE) * 2 + (position & (SLICE - 1))


def gathered(sc, ref, at, count, t):
    return jnp.concatenate([ref[sc[at + i], :, t].reshape(HALF, HD) for i in range(count)], 0)


def query_tile(sc, q, first, tile):
    at = first + tile * QB
    q0, q1, q2 = (gathered(sc, q, INDEX + at, QB, t) for t in range(3))
    row = lax.broadcasted_iota(jnp.int32, (QT, HD), 0)
    qpos = lookup(sc, BASE + at, QB, row, HALF) + within(row)
    start = jnp.zeros_like(qpos)
    for d in range(3):
        start = jnp.where(qpos >= sc[STARTS + d], sc[STARTS + d], start)
    return q0, jnp.concatenate([q1, q0], 1), jnp.concatenate([q2, q0], 1), qpos, start


def see(sc, kv, first, queries, state, low, high, room):
    q0, q10, q20, qpos, start = queries
    col = lax.broadcasted_iota(jnp.int32, (1, KT), 1)
    ones = jnp.ones((KT, HD), jnp.bfloat16)

    top_ref, acc_ref, acc_w_ref = room
    top_ref[...], acc_ref[...], acc_w_ref[...] = state

    def step(kt, _):
        top = top_ref[...]
        at = first + kt * KB
        k0, k1, k2, v0, v1, v2 = (gathered(sc, kv, INDEX + at, KB, t) for t in range(6))
        kpos = lookup(sc, BASE + at, KB, col, HALF) + within(col)
        s = lax.dot_general(q0, k0, NT, preferred_element_type=jnp.float32)
        d1 = lax.dot_general(q10, jnp.concatenate([k0, k1], 1), NT, preferred_element_type=jnp.float32)
        d2 = lax.dot_general(q20, jnp.concatenate([k0, k2], 1), NT, preferred_element_type=jnp.float32)
        parts = []
        for i in range(KT // HD):
            lanes = slice(i * HD, i * HD + HD)
            visible = (kpos[:, lanes] <= qpos) & (kpos[:, lanes] >= start)
            parts.append(jnp.where(visible, s[:, lanes], HIDDEN))
        peak = functools.reduce(jnp.maximum, parts)
        new = jnp.maximum(top, jnp.max(peak, axis=1, keepdims=True))
        shrink = jnp.exp2((top - new) * EXPONENT)
        shift = jnp.where(new < 0.5 * HIDDEN, 0.0, new)
        e = jnp.concatenate([jnp.exp2((part - shift) * EXPONENT) for part in parts], 1)
        w = jnp.concatenate([(e * d1).astype(jnp.bfloat16), (e * d2).astype(jnp.bfloat16)], 0)
        shrink4 = jnp.concatenate([shrink] * 4, 1)
        shrink2 = shrink4[:, : 2 * HD]
        top_ref[...] = new
        acc_ref[...] = acc_ref[...] * shrink4 + jnp.dot(
            e.astype(jnp.bfloat16), jnp.concatenate([v0, v1, v2, ones], 1), preferred_element_type=jnp.float32
        )
        acc_w_ref[...] = acc_w_ref[...] * jnp.concatenate([shrink2, shrink2], 0) + jnp.dot(
            w, jnp.concatenate([v0, ones], 1), preferred_element_type=jnp.float32
        )
        return 0

    lax.fori_loop(low, high, step, 0)
    return top_ref[...], acc_ref[...], acc_w_ref[...]


def fresh():
    return (
        jnp.full((QT, HD), HIDDEN, jnp.float32),
        jnp.zeros((QT, 4 * HD), jnp.float32),
        jnp.zeros((2 * QT, 2 * HD), jnp.float32),
    )


def pack_state(state):
    top, acc, acc_w = state
    total, c1, c2 = acc[:, 3 * HD :], acc_w[:QT, HD:] * SCALE, acc_w[QT:, HD:] * SCALE
    lane = lax.broadcasted_iota(jnp.int32, (QT, HD), 1)
    stats = jnp.where(lane == 0, top, jnp.where(lane == 1, total, jnp.where(lane == 2, c1, c2)))
    return (
        acc[:, :HD],
        acc[:, HD : 2 * HD] + acc_w[:QT, :HD] * SCALE,
        acc[:, 2 * HD : 3 * HD] + acc_w[QT:, :HD] * SCALE,
        stats,
    )


def unpack_state(parts):
    a, g1, g2, stats = parts
    top, total, c1, c2 = (jnp.broadcast_to(stats[:, i : i + 1], (QT, HD)) for i in range(4))
    zero = jnp.zeros((QT, HD), jnp.float32)
    acc = jnp.concatenate([a, g1, g2, total], 1)
    c = jnp.concatenate([c1, c2], 0) * (1.0 / SCALE)
    return top, acc, jnp.concatenate([jnp.concatenate([zero, zero], 0), c], 1)


def join_states(one, two):
    top = jnp.maximum(one[0], two[0])
    f, g = (jnp.exp2((t - top) * EXPONENT) for t in (one[0], two[0]))
    f4, g4 = (jnp.concatenate([v] * 4, 1) for v in (f, g))
    f2, g2 = (jnp.concatenate([v[:, : 2 * HD]] * 2, 0) for v in (f4, g4))
    return top, one[1] * f4 + two[1] * g4, one[2] * f2 + two[2] * g2


def gather_state(sc, ref, at):
    return unpack_state([gathered(sc, ref, at, QB, t) for t in range(4)])


ROOM = (
    pltpu.VMEM((QT, HD), jnp.float32),
    pltpu.VMEM((QT, 4 * HD), jnp.float32),
    pltpu.VMEM((2 * QT, 2 * HD), jnp.float32),
)


def copy_in(pairs, sem):
    copies = [pltpu.make_async_copy(src, dst, sem) for src, dst in pairs]
    for copy in copies:
        copy.start()
    for copy in copies:
        copy.wait()


def kernel_state(rows):
    return pltpu.VMEM((rows, 2, 4, SLICE, HD), jnp.float32)


def key_scratch(planes):
    return pltpu.VMEM((planes * 8, 2, 6, SLICE, HD), jnp.bfloat16)


def plane_copies(refs, kv):
    return [(ref, kv.at[4 * i : 4 * i + 4]) for i, ref in enumerate(refs)]


def estimate(queries, keys):
    pairs = queries * keys // 4
    return pl.CostEstimate(flops=pairs * 2560, bytes_accessed=8 * 2**20, transcendentals=pairs)


def attend(sc, queries, planes, key_set, held=()):
    n = len(planes)

    def kernel(sc, q_own, q_other, *refs):
        kv_refs, refs = refs[:n], refs[n:]
        held_refs, refs = refs[: len(held)], refs[len(held) :]
        out_refs, (kv, q, st, sem, *room) = refs[:2], refs[2:]
        before = [(ref, st.at[8 * i : 8 * i + 8]) for i, ref in enumerate(held_refs)]
        copy_in([(q_own, q.at[0:8]), (q_other, q.at[8:16]), *before, *plane_copies(kv_refs, kv)], sem)

        def tile(qt, _):
            at = INDEX + FIRST[ALL] + qt * QB
            low, high = sc[LOW + key_set * 6 + qt], sc[HIGH + key_set * 6 + qt]

            def work():
                info = query_tile(sc, q, FIRST[ALL], qt)
                state = gather_state(sc, st, at) if held else fresh()
                parts = pack_state(see(sc, kv, FIRST[key_set], info, state, low, high, room))
                for i in range(QB):
                    for t in range(4):
                        st[sc[at + i], :, t] = parts[t][i * HALF : i * HALF + HALF].reshape(2, SLICE, HD)

            if held:
                pl.when(high > low)(work)
            else:
                work()
            return 0

        lax.fori_loop(0, 4, tile, 0)
        copy_in([(st.at[8 * i : 8 * i + 8], ref) for i, ref in enumerate(out_refs)], sem)

    part = jax.ShapeDtypeStruct((8, 2, 4, SLICE, HD), jnp.float32)
    return pl.pallas_call(
        kernel,
        out_shape=(part, part),
        in_specs=[SMEM] + [ANY] * (2 + n + len(held)),
        out_specs=(ANY, ANY),
        scratch_shapes=[
            key_scratch(n // 2),
            pltpu.VMEM((16, 2, 3, SLICE, HD), jnp.bfloat16),
            kernel_state(16),
            pltpu.SemaphoreType.DMA,
            *ROOM,
        ],
        compiler_params=pltpu.CompilerParams(vmem_limit_bytes=GRANT),
        cost_estimate=estimate(1024, n // 2 * 512),
    )(sc, *queries, *planes, *held)


def finish(sc, query, planes, held):
    n = len(planes)

    def kernel(sc, q_ref, *refs):
        kv_refs, held_refs = refs[:n], refs[n : n + 2]
        out, kv, q, one, two, sem, *room = refs[n + 2 :]
        copy_in([(q_ref, q), (held_refs[0], one), (held_refs[1], two), *plane_copies(kv_refs, kv)], sem)

        def tile(qt, _):
            at = INDEX + FIRST[OWN] + qt * QB
            info = query_tile(sc, q, FIRST[OWN], qt)
            state = join_states(gather_state(sc, one, at), gather_state(sc, two, at))
            low, high = sc[LOW + LAST * 6 + 4 + qt], sc[HIGH + LAST * 6 + 4 + qt]
            parts = results(see(sc, kv, FIRST[LAST], info, state, low, high, room))
            for i in range(QB):
                for t, part in enumerate(parts):
                    block = part[i * HALF : i * HALF + HALF].reshape(2, SLICE, HD)
                    out[sc[at + i], :, t] = block.astype(jnp.bfloat16)
            return 0

        lax.fori_loop(0, 2, tile, 0)

    return pl.pallas_call(
        kernel,
        out_shape=jax.ShapeDtypeStruct((8, 2, 3, SLICE, HD), jnp.bfloat16),
        in_specs=[SMEM] + [ANY] * (3 + n),
        out_specs=VMEM,
        scratch_shapes=[
            key_scratch(n // 2),
            pltpu.VMEM((8, 2, 3, SLICE, HD), jnp.bfloat16),
            kernel_state(8),
            kernel_state(8),
            pltpu.SemaphoreType.DMA,
            *ROOM,
        ],
        compiler_params=pltpu.CompilerParams(vmem_limit_bytes=GRANT),
        cost_estimate=estimate(512, n // 2 * 512),
    )(sc, query, *planes, *held)


def results(state):
    _, acc, acc_w = state
    inv = 1.0 / acc[:, 3 * HD :]
    primal = acc[:, :HD] * inv
    parts = [primal]
    for i in (1, 2):
        mine = slice((i - 1) * QT, i * QT)
        grad = acc[:, i * HD : (i + 1) * HD] + acc_w[mine, :HD] * SCALE
        parts.append(grad * inv - (acc_w[mine, HD:] * SCALE * inv) * primal)
    return parts


def hop(block, direction):
    return lax.ppermute(block, Z, [(i, (i + direction) % NZ) for i in range(NZ)])


def swap_cores(block):
    return lax.ppermute(block, "c", [(0, 1), (1, 0)])


def shards(query_set, key_set, value_set, block_order, documents):
    kv = lax.all_to_all(split_heads(key_set, value_set), XY, 0, 0).reshape(8, 2, 6, SLICE, HD)
    sc = scalars(block_order, documents, *(lax.axis_index(a) for a in ("zh", "zl", "c")))
    kv, q, sc = lax.optimization_barrier((kv, split_heads(query_set), sc))
    q = lax.all_to_all(q, XY, 0, 0).reshape(8, 2, 3, SLICE, HD)
    planes = {0: [kv[:4], kv[4:]]}

    def advance(step):
        planes[-step] = [hop(p, 1) for p in planes[1 - step]]
        planes[step] = [hop(p, -1) for p in planes[step - 1]]

    def attend_set(i, held=()):
        return attend(sc, queries, [p for o in SETS[i] for p in planes[o]], i, held)

    advance(1)
    advance(2)
    queries = (q, swap_cores(q))
    state = attend_set(0)
    state, planes[-2][1], planes[2][0] = lax.optimization_barrier((state, planes[-2][1], planes[2][0]))
    advance(3)
    state = attend_set(1, state)
    state, planes[-3][0], planes[3][1] = lax.optimization_barrier((state, planes[-3][0], planes[3][1]))
    far = [hop(planes[-3][0], 1), hop(planes[3][1], -1)]
    own, other = attend_set(2, state)
    own, other, far = lax.optimization_barrier((own, other, far))
    done = finish(sc, q, [*far, *map(swap_cores, far)], (own, swap_cores(other)))
    done = lax.all_to_all(done.reshape(HEADS, 3, SLICE, HD), XY, 0, 0)
    return join_heads(done)


def solution(mesh):
    fine = Mesh(mesh.devices.reshape(SIZES), NAMES)
    rows = P(None, NAMES, None)
    return jax.shard_map(
        shards,
        mesh=fine,
        in_specs=(rows, rows, rows, P(), P()),
        out_specs=rows,
        check_vma=False,
    )
```

```python
import functools

import jax
import jax.numpy as jnp
from jax import lax
from jax.experimental import pallas as pl
from jax.experimental.pallas import tpu as pltpu
from jax.sharding import Mesh
from jax.sharding import PartitionSpec as P

HD = 128
HEADS = 16
BLOCK = 128
SLICE = 32
HALF = 2 * SLICE
Z = ("zh", "zl")
XY = ("y", "xh", "xl")
NAMES = ("zh", "y", "c", "xh", "xl", "zl")
SIZES = (4, 4, 2, 2, 2, 2)
NZ = 8
SCALE = 1.0 / HD**0.5
EXPONENT = SCALE * 1.4426950408889634
HIDDEN = -1e30
GRANT = 16 * 2**20
VMEM = pl.BlockSpec(memory_space=pltpu.VMEM)
SMEM = pl.BlockSpec(memory_space=pltpu.SMEM)
ANY = pl.BlockSpec(memory_space=pl.ANY)
NT = (((1,), (1,)), ((), ()))

SETS = ((-1, 0, 1), (-2, 2), (-3, 3), (4,))
LAST = 3
ALL, OWN = 4, 5
FIRST = (0, 24, 40, 56, 72, 88)
N_SLOTS = 96
QB, KB = 4, 8
QT, KT = QB * HALF, KB * HALF
INDEX, BASE, LOW, HIGH, STARTS = 0, 96, 192, 216, 240


def split_heads(*arrays):
    def kernel(*refs):
        out = refs[-1]
        for h in range(HEADS):
            for a, ref in enumerate(refs[:-1]):
                out[h, 3 * a : 3 * a + 3] = ref[:, :, h * HD : (h + 1) * HD]

    return pl.pallas_call(
        kernel,
        out_shape=jax.ShapeDtypeStruct((HEADS, 3 * len(arrays), SLICE, HD), jnp.bfloat16),
        in_specs=[VMEM] * len(arrays),
        out_specs=VMEM,
    )(*arrays)


def join_heads(parts):
    def kernel(ref, out):
        for h in range(HEADS):
            out[:, :, h * HD : (h + 1) * HD] = ref[h]

    return pl.pallas_call(
        kernel,
        out_shape=jax.ShapeDtypeStruct((3, SLICE, HEADS * HD), jnp.bfloat16),
        in_specs=[VMEM],
        out_specs=VMEM,
    )(parts)


def scalars(order, documents, zh, zl, c):
    i32 = jnp.int32
    z = zh * 2 + zl
    rows = [(o, 0, i) for i in range(LAST) for o in SETS[i]]
    rows += [(o, other, LAST) for other in range(2) for o in SETS[LAST]]
    rows += [(0, 0, ALL), (0, 1, ALL), (0, 0, OWN)]
    offsets, cores, sets = (jnp.array(v, i32) for v in zip(*rows, strict=True))
    begins = jnp.array([FIRST[r[2]] // 8 for r in rows], i32)
    planes = lax.rem(z + offsets + NZ, NZ)
    table = order.reshape(4, 4, 2, 2).transpose(0, 2, 1, 3).reshape(8, 8)
    line = planes // 2 * 2 + lax.rem(cores + c, 2)
    hit = line[:, None] == jnp.arange(8, dtype=i32)[None, :]
    pos = jnp.sum(jnp.where(hit[:, :, None], table[None], 0), axis=1)
    code = (sets[:, None] * 4096 + pos * 2 + lax.rem(planes, 2)[:, None]).reshape(-1)
    payload = ((jnp.arange(len(rows), dtype=i32) - begins)[:, None] * 8 + jnp.arange(8, dtype=i32)[None, :]).reshape(-1)
    rank = jnp.sum((code[None, :] < code[:, None]).astype(i32), axis=1)
    slot = jnp.arange(N_SLOTS, dtype=i32)
    hits = rank[None, :] == slot[:, None]
    index = jnp.sum(jnp.where(hits, payload[None, :], 0), axis=1)
    low_bits = code % 4096
    base_of = low_bits // 2 * BLOCK + low_bits % 2 * SLICE
    base = jnp.sum(jnp.where(hits, base_of[None, :], 0), axis=1)
    starts = jnp.sum((documents[None, :] < jnp.arange(1, 4, dtype=i32)[:, None]).astype(i32), axis=1)
    first = base[FIRST[ALL] :: QB]
    last = base[FIRST[ALL] + QB - 1 :: QB] + BLOCK - SLICE
    begin = jnp.max(jnp.where(starts[None, :] <= first[:, None], starts[None, :], 0), axis=1)
    set_of = code // 4096
    member = set_of[None, None, :] == jnp.arange(len(SETS), dtype=i32)[:, None, None]
    before = base_of[None, None, :] + BLOCK - SLICE <= begin[None, :, None]
    upto = base_of[None, None, :] < last[None, :, None]
    low = jnp.sum((member & before).astype(i32), axis=2) // KB
    high = (jnp.sum((member & upto).astype(i32), axis=2) + KB - 1) // KB
    return jnp.concatenate([index, base, low.reshape(-1), high.reshape(-1), starts])


def lookup(sc, at, count, position, size):
    out = sc[at]
    for i in range(1, count):
        out = jnp.where(position >= i * size, sc[at + i], out)
    return out


def within(position):
    return (position & SLICE) * 2 + (position & (SLICE - 1))


def gathered(sc, ref, at, count, t):
    return jnp.concatenate([ref[sc[at + i], :, t].reshape(HALF, HD) for i in range(count)], 0)


def query_tile(sc, q, first, tile):
    at = first + tile * QB
    q0, q1, q2 = (gathered(sc, q, INDEX + at, QB, t) for t in range(3))
    row = lax.broadcasted_iota(jnp.int32, (QT, HD), 0)
    qpos = lookup(sc, BASE + at, QB, row, HALF) + within(row)
    start = jnp.zeros_like(qpos)
    for d in range(3):
        start = jnp.where(qpos >= sc[STARTS + d], sc[STARTS + d], start)
    return q0, jnp.concatenate([q1, q0], 1), jnp.concatenate([q2, q0], 1), qpos, start


def see(sc, kv, first, queries, state, low, high, room):
    q0, q10, q20, qpos, start = queries
    col = lax.broadcasted_iota(jnp.int32, (1, KT), 1)
    ones = jnp.ones((KT, HD), jnp.bfloat16)

    top_ref, acc_ref, acc_w_ref = room
    top_ref[...], acc_ref[...], acc_w_ref[...] = state

    def step(kt, _):
        top = top_ref[...]
        at = first + kt * KB
        k0, k1, k2, v0, v1, v2 = (gathered(sc, kv, INDEX + at, KB, t) for t in range(6))
        kpos = lookup(sc, BASE + at, KB, col, HALF) + within(col)
        s = lax.dot_general(q0, k0, NT, preferred_element_type=jnp.float32)
        d1 = lax.dot_general(q10, jnp.concatenate([k0, k1], 1), NT, preferred_element_type=jnp.float32)
        d2 = lax.dot_general(q20, jnp.concatenate([k0, k2], 1), NT, preferred_element_type=jnp.float32)
        parts = []
        for i in range(KT // HD):
            lanes = slice(i * HD, i * HD + HD)
            visible = (kpos[:, lanes] <= qpos) & (kpos[:, lanes] >= start)
            parts.append(jnp.where(visible, s[:, lanes], HIDDEN))
        peak = functools.reduce(jnp.maximum, parts)
        new = jnp.maximum(top, jnp.max(peak, axis=1, keepdims=True))
        shrink = jnp.exp2((top - new) * EXPONENT)
        shift = jnp.where(new < 0.5 * HIDDEN, 0.0, new)
        e = jnp.concatenate([jnp.exp2((part - shift) * EXPONENT) for part in parts], 1)
        w = jnp.concatenate([(e * d1).astype(jnp.bfloat16), (e * d2).astype(jnp.bfloat16)], 0)
        shrink4 = jnp.concatenate([shrink] * 4, 1)
        shrink2 = shrink4[:, : 2 * HD]
        top_ref[...] = new
        acc_ref[...] = acc_ref[...] * shrink4 + jnp.dot(
            e.astype(jnp.bfloat16), jnp.concatenate([v0, v1, v2, ones], 1), preferred_element_type=jnp.float32
        )
        acc_w_ref[...] = acc_w_ref[...] * jnp.concatenate([shrink2, shrink2], 0) + jnp.dot(
            w, jnp.concatenate([v0, ones], 1), preferred_element_type=jnp.float32
        )
        return 0

    lax.fori_loop(low, high, step, 0)
    return top_ref[...], acc_ref[...], acc_w_ref[...]


def fresh():
    return (
        jnp.full((QT, HD), HIDDEN, jnp.float32),
        jnp.zeros((QT, 4 * HD), jnp.float32),
        jnp.zeros((2 * QT, 2 * HD), jnp.float32),
    )


def pack_state(state):
    top, acc, acc_w = state
    total, c1, c2 = acc[:, 3 * HD :], acc_w[:QT, HD:] * SCALE, acc_w[QT:, HD:] * SCALE
    lane = lax.broadcasted_iota(jnp.int32, (QT, HD), 1)
    stats = jnp.where(lane == 0, top, jnp.where(lane == 1, total, jnp.where(lane == 2, c1, c2)))
    return (
        acc[:, :HD],
        acc[:, HD : 2 * HD] + acc_w[:QT, :HD] * SCALE,
        acc[:, 2 * HD : 3 * HD] + acc_w[QT:, :HD] * SCALE,
        stats,
    )


def unpack_state(parts):
    a, g1, g2, stats = parts
    top, total, c1, c2 = (jnp.broadcast_to(stats[:, i : i + 1], (QT, HD)) for i in range(4))
    zero = jnp.zeros((QT, HD), jnp.float32)
    acc = jnp.concatenate([a, g1, g2, total], 1)
    c = jnp.concatenate([c1, c2], 0) * (1.0 / SCALE)
    return top, acc, jnp.concatenate([jnp.concatenate([zero, zero], 0), c], 1)


def join_states(one, two):
    top = jnp.maximum(one[0], two[0])
    f, g = (jnp.exp2((t - top) * EXPONENT) for t in (one[0], two[0]))
    f4, g4 = (jnp.concatenate([v] * 4, 1) for v in (f, g))
    f2, g2 = (jnp.concatenate([v[:, : 2 * HD]] * 2, 0) for v in (f4, g4))
    return top, one[1] * f4 + two[1] * g4, one[2] * f2 + two[2] * g2


def gather_state(sc, ref, at):
    return unpack_state([gathered(sc, ref, at, QB, t) for t in range(4)])


ROOM = (
    pltpu.VMEM((QT, HD), jnp.float32),
    pltpu.VMEM((QT, 4 * HD), jnp.float32),
    pltpu.VMEM((2 * QT, 2 * HD), jnp.float32),
)


def copy_in(pairs, sem):
    copies = [pltpu.make_async_copy(src, dst, sem) for src, dst in pairs]
    for copy in copies:
        copy.start()
    for copy in copies:
        copy.wait()


def kernel_state(rows):
    return pltpu.VMEM((rows, 2, 4, SLICE, HD), jnp.float32)


def key_scratch(planes):
    return pltpu.VMEM((planes * 8, 2, 6, SLICE, HD), jnp.bfloat16)


def plane_copies(refs, kv):
    return [(ref, kv.at[4 * i : 4 * i + 4]) for i, ref in enumerate(refs)]


def estimate(queries, keys):
    pairs = queries * keys // 4
    return pl.CostEstimate(flops=pairs * 2560, bytes_accessed=8 * 2**20, transcendentals=pairs)


def attend(sc, queries, planes, key_set, held=()):
    n = len(planes)

    def kernel(sc, q_own, q_other, *refs):
        kv_refs, refs = refs[:n], refs[n:]
        held_refs, refs = refs[: len(held)], refs[len(held) :]
        out_refs, (kv, q, st, sem, *room) = refs[:2], refs[2:]
        before = [(ref, st.at[8 * i : 8 * i + 8]) for i, ref in enumerate(held_refs)]
        copy_in([(q_own, q.at[0:8]), (q_other, q.at[8:16]), *before, *plane_copies(kv_refs, kv)], sem)

        def tile(qt, _):
            at = INDEX + FIRST[ALL] + qt * QB
            low, high = sc[LOW + key_set * 6 + qt], sc[HIGH + key_set * 6 + qt]

            def work():
                info = query_tile(sc, q, FIRST[ALL], qt)
                state = gather_state(sc, st, at) if held else fresh()
                parts = pack_state(see(sc, kv, FIRST[key_set], info, state, low, high, room))
                for i in range(QB):
                    for t in range(4):
                        st[sc[at + i], :, t] = parts[t][i * HALF : i * HALF + HALF].reshape(2, SLICE, HD)

            if held:
                pl.when(high > low)(work)
            else:
                work()
            return 0

        lax.fori_loop(0, 4, tile, 0)
        copy_in([(st.at[8 * i : 8 * i + 8], ref) for i, ref in enumerate(out_refs)], sem)

    part = jax.ShapeDtypeStruct((8, 2, 4, SLICE, HD), jnp.float32)
    return pl.pallas_call(
        kernel,
        out_shape=(part, part),
        in_specs=[SMEM] + [ANY] * (2 + n + len(held)),
        out_specs=(ANY, ANY),
        scratch_shapes=[
            key_scratch(n // 2),
            pltpu.VMEM((16, 2, 3, SLICE, HD), jnp.bfloat16),
            kernel_state(16),
            pltpu.SemaphoreType.DMA,
            *ROOM,
        ],
        compiler_params=pltpu.CompilerParams(vmem_limit_bytes=GRANT),
        cost_estimate=estimate(1024, n // 2 * 512),
    )(sc, *queries, *planes, *held)


def finish(sc, query, planes, held):
    n = len(planes)

    def kernel(sc, q_ref, *refs):
        kv_refs, held_refs = refs[:n], refs[n : n + 2]
        out, kv, q, one, two, sem, *room = refs[n + 2 :]
        copy_in([(q_ref, q), (held_refs[0], one), (held_refs[1], two), *plane_copies(kv_refs, kv)], sem)

        def tile(qt, _):
            at = INDEX + FIRST[OWN] + qt * QB
            info = query_tile(sc, q, FIRST[OWN], qt)
            state = join_states(gather_state(sc, one, at), gather_state(sc, two, at))
            low, high = sc[LOW + LAST * 6 + 4 + qt], sc[HIGH + LAST * 6 + 4 + qt]
            parts = results(see(sc, kv, FIRST[LAST], info, state, low, high, room))
            for i in range(QB):
                for t, part in enumerate(parts):
                    block = part[i * HALF : i * HALF + HALF].reshape(2, SLICE, HD)
                    out[sc[at + i], :, t] = block.astype(jnp.bfloat16)
            return 0

        lax.fori_loop(0, 2, tile, 0)

    return pl.pallas_call(
        kernel,
        out_shape=jax.ShapeDtypeStruct((8, 2, 3, SLICE, HD), jnp.bfloat16),
        in_specs=[SMEM] + [ANY] * (3 + n),
        out_specs=VMEM,
        scratch_shapes=[
            key_scratch(n // 2),
            pltpu.VMEM((8, 2, 3, SLICE, HD), jnp.bfloat16),
            kernel_state(8),
            kernel_state(8),
            pltpu.SemaphoreType.DMA,
            *ROOM,
        ],
        compiler_params=pltpu.CompilerParams(vmem_limit_bytes=GRANT),
        cost_estimate=estimate(512, n // 2 * 512),
    )(sc, query, *planes, *held)


def results(state):
    _, acc, acc_w = state
    inv = 1.0 / acc[:, 3 * HD :]
    primal = acc[:, :HD] * inv
    parts = [primal]
    for i in (1, 2):
        mine = slice((i - 1) * QT, i * QT)
        grad = acc[:, i * HD : (i + 1) * HD] + acc_w[mine, :HD] * SCALE
        parts.append(grad * inv - (acc_w[mine, HD:] * SCALE * inv) * primal)
    return parts


def hop(block, direction):
    return lax.ppermute(block, Z, [(i, (i + direction) % NZ) for i in range(NZ)])


def swap_cores(block):
    return lax.ppermute(block, "c", [(0, 1), (1, 0)])


def shards(query_set, key_set, value_set, block_order, documents):
    kv = lax.all_to_all(split_heads(key_set, value_set), XY, 0, 0).reshape(8, 2, 6, SLICE, HD)
    sc = scalars(block_order, documents, *(lax.axis_index(a) for a in ("zh", "zl", "c")))
    kv, packed, sc = lax.optimization_barrier((kv, split_heads(query_set), sc))
    planes = {0: [kv[:4], kv[4:]]}

    def advance(step):
        planes[-step] = [hop(p, 1) for p in planes[1 - step]]
        planes[step] = [hop(p, -1) for p in planes[step - 1]]

    def attend_set(i, held=()):
        return attend(sc, queries, [p for o in SETS[i] for p in planes[o]], i, held)

    advance(1)
    packed, planes[-1][1] = lax.optimization_barrier((packed, planes[-1][1]))
    q = lax.all_to_all(packed, XY, 0, 0).reshape(8, 2, 3, SLICE, HD)
    advance(2)
    queries = (q, swap_cores(q))
    state = attend_set(0)
    state, planes[-2][1], planes[2][0] = lax.optimization_barrier((state, planes[-2][1], planes[2][0]))
    advance(3)
    state = attend_set(1, state)
    state, planes[-3][0], planes[3][1] = lax.optimization_barrier((state, planes[-3][0], planes[3][1]))
    far = [hop(planes[-3][0], 1), hop(planes[3][1], -1)]
    own, other = attend_set(2, state)
    own, other, far = lax.optimization_barrier((own, other, far))
    done = finish(sc, q, [*far, *map(swap_cores, far)], (own, swap_cores(other)))
    done = lax.all_to_all(done.reshape(HEADS, 3, SLICE, HD), XY, 0, 0)
    return join_heads(done)


def solution(mesh):
    fine = Mesh(mesh.devices.reshape(SIZES), NAMES)
    rows = P(None, NAMES, None)
    return jax.shard_map(
        shards,
        mesh=fine,
        in_specs=(rows, rows, rows, P(), P()),
        out_specs=rows,
        check_vma=False,
    )
```
